128 devices in a mesh: replica: 8 (over z_lo, y), fsdp: 16 (over z_hi, x, core).
Axes of the slice: x: 4, y: 4, z: 4 (z_hi: 2, z_lo: 2; z = z_hi * 2 + z_lo), core: 2. Of those that a mesh axis runs over, the one named last changes fastest.
Arguments:
- tokens: bfloat16 [65536, 8192], P(('replica', 'fsdp')), may hold values from -6 to 6
- kv_weight: bfloat16 [8, 8192, 1024], P('replica', 'fsdp'), may hold values from -0.0625 to 0.0625
- norm_gain: bfloat16 [8, 8192], P('replica', 'fsdp'), may hold values from 0.099609375 to 1.8984375
- cotangent: bfloat16 [65536, 1024], P(('replica', 'fsdp')), may hold values from -6 to 6
- global_params: float32 [4, 1024, 1024], P(None, 'fsdp'), may hold values from -6 to 6
- momentum: float32 [4, 1024, 1024], P(None, 'fsdp'), may hold values from -3 to 3
- local_params: float32 [8, 1024, 1024], P('replica', 'fsdp'), may hold values from -6 to 6
- fragment_order: int32 [4], replicated, may hold values from 0 to 3, each once
Outputs:
- keys_values: bfloat16 [65536, 1024], P(('replica', 'fsdp'))
- input_grad: bfloat16 [65536, 8192], P(('replica', 'fsdp'))
- weight_grad: float32 [8, 8192, 1024], P('replica', 'fsdp')
- gain_grad: float32 [8, 8192], P('replica', 'fsdp')
- new_params: float32 [4, 1024, 1024], P(None, 'fsdp')
- new_momentum: float32 [4, 1024, 1024], P(None, 'fsdp')
The draws below stay inside these ranges and needn't reach their ends.
Inputs may be any that keep to these rules, and one draw needn't show every extreme that they name: `fragment_order`: each fragment number appears once; the first entry names the fragment synchronized in this step.
All inputs are finite; a program needn't handle non-finite values.
Results may differ from the reference program's by a relative error of at most 0.025.
Values may be sent and summed in bfloat16 or wider, within the bound.
A program may use at most 192 MiB of HBM per device.

```python
import jax
import jax.numpy as jnp
from jax import lax

D = 8192
TOK_DEV = 512
FRAGS = 4
FRAG_COLS = 1024
KVC = 512
REPLICAS = 8
TOKENS = 65536
FRAG_ROWS = 1024
N_FSDP = 16


def shard_levels(stream_key, extent, cuts, smallest, high):
    factor_of = 1.0
    for dim, shards_of in cuts:
        steps = jax.random.uniform(jax.random.fold_in(jax.random.fold_in(stream_key, 6), dim), (shards_of,), jnp.float32, smallest / len(cuts), high / len(cuts))
        factor_of = factor_of * jnp.repeat(jnp.exp(steps), extent[dim] // shards_of).reshape((-1,) + (1,) * (len(extent) - 1 - dim))
    return factor_of


def gaussian(rng, shape, scale, most, pieces=(), dtype=jnp.bfloat16):
    drawn = scale * jax.random.normal(rng, shape, jnp.float32)
    if pieces:
        drawn = drawn * shard_levels(rng, shape, pieces, -0.22, 0.18)
    return jnp.clip(drawn, -most, most).astype(dtype)


def setup_inputs(seed: int = 0) -> dict:
    key_list = jax.random.split(jax.random.key(seed), 9)
    return {
        "tokens": gaussian(key_list[0], (TOKENS, D), 1.0, 6.0, ((0, 128),)),
        "kv_weight": gaussian(key_list[1], (REPLICAS, D, 2 * KVC), D ** -0.5, 0.0625, ((0, 8), (1, 16))),
        "norm_gain": jnp.clip(1.0 + 0.18 * jax.random.normal(key_list[2], (REPLICAS, D), jnp.float32), 0.099609375, 1.8984375).astype(jnp.bfloat16),
        "cotangent": gaussian(key_list[3], (TOKENS, 2 * KVC), 1.0, 6.0, ((0, 128),)),
        "global_params": gaussian(key_list[4], (FRAGS, FRAG_ROWS, FRAG_COLS), 1.0, 6.0, ((1, 16),), jnp.float32),
        "momentum": gaussian(key_list[5], (FRAGS, FRAG_ROWS, FRAG_COLS), 0.5, 3.0, ((1, 16),), jnp.float32),
        "local_params": gaussian(key_list[6], (REPLICAS, FRAG_ROWS, FRAG_COLS), 1.0, 6.0, ((0, 8), (1, 16)), jnp.float32),
        "fragment_order": jax.random.permutation(key_list[7], FRAGS).astype(jnp.int32),
    }


epsilon = 1e-05
outer_beta = 0.9
outer_rate = 0.7

def replica_pass(tokens, weight, gain, cotangent):
    widened = tokens.astype(jnp.float32)
    inverse_rms = lax.rsqrt(lax.optimization_barrier(jnp.mean(widened * widened, axis=1, keepdims=True)) + epsilon)
    scaled = widened * inverse_rms
    gain_wide = gain.astype(jnp.float32)
    normed = (scaled * gain_wide).astype(jnp.bfloat16)
    keys_values = jnp.dot(normed, weight, preferred_element_type=jnp.float32).astype(jnp.bfloat16)
    back = jnp.dot(cotangent, weight.T, preferred_element_type=jnp.float32)
    weighted = gain_wide * back
    row_sums = lax.optimization_barrier(jnp.sum(weighted * scaled, axis=1, keepdims=True))
    input_grad = (inverse_rms * (weighted - scaled * (row_sums / D))).astype(jnp.bfloat16)
    normed_blocks = normed.reshape(N_FSDP, TOK_DEV, D)
    cot_blocks = cotangent.reshape(N_FSDP, TOK_DEV, 2 * KVC)
    back_blocks = back.reshape(N_FSDP, TOK_DEV, D)
    scaled_blocks = scaled.reshape(N_FSDP, TOK_DEV, D)

    def block_terms(summed, block):
        normed_block, cot_block, back_block, scaled_block = block
        grad_term = jnp.dot(normed_block.T, cot_block, preferred_element_type=jnp.float32)
        gain_term = lax.optimization_barrier(jnp.sum(back_block * scaled_block, axis=0))
        grad_low, gain_low = lax.optimization_barrier((grad_term.astype(jnp.bfloat16), gain_term.astype(jnp.bfloat16)))
        return ((summed[0] + grad_low.astype(jnp.float32), summed[1] + gain_low.astype(jnp.float32)), None)
    initial = (jnp.zeros((D, 2 * KVC), jnp.float32), jnp.zeros((D,), jnp.float32))
    (weight_grad, gain_grad), _ = lax.scan(block_terms, initial, (normed_blocks, cot_blocks, back_blocks, scaled_blocks))
    return (keys_values, input_grad, weight_grad, gain_grad)

def reference(tokens, kv_weight, norm_gain, cotangent, global_params, momentum, local_params, fragment_order):
    replica_rows = TOK_DEV * N_FSDP
    kv_parts, input_parts, weight_parts, gain_parts = ([], [], [], [])
    for replica in range(REPLICAS):
        lower = replica * replica_rows
        upper = lower + replica_rows
        result = replica_pass(tokens[lower:upper], kv_weight[replica], norm_gain[replica], cotangent[lower:upper])
        kv_parts.append(result[0])
        input_parts.append(result[1])
        weight_parts.append(result[2])
        gain_parts.append(result[3])
    keys_values = jnp.concatenate(kv_parts, axis=0)
    input_grad = jnp.concatenate(input_parts, axis=0)
    weight_grad = jnp.stack(weight_parts, axis=0)
    gain_grad = jnp.stack(gain_parts, axis=0)
    fragment_slot = fragment_order[0].astype(jnp.int32)
    current = lax.dynamic_index_in_dim(global_params, fragment_slot, 0, keepdims=False)
    moment_old = lax.dynamic_index_in_dim(momentum, fragment_slot, 0, keepdims=False)
    averaged = lax.optimization_barrier(jnp.sum(current[None] - local_params, axis=0)) / REPLICAS
    moment = outer_beta * moment_old + averaged
    updated = current - outer_rate * (averaged + outer_beta * moment)
    new_params = lax.dynamic_update_index_in_dim(global_params, updated, fragment_slot, 0)
    new_momentum = lax.dynamic_update_index_in_dim(momentum, moment, fragment_slot, 0)
    return (keys_values, input_grad, weight_grad, gain_grad, new_params, new_momentum)
```

```python
import functools

import jax
import jax.numpy as jnp
from jax import lax
from jax.experimental import pallas as pl
from jax.experimental.pallas import tpu as pltpu
from jax.sharding import PartitionSpec as P

epsilon = 1e-05
outer_beta = 0.9
outer_rate = 0.7
f32 = jnp.float32
bf16 = jnp.bfloat16
MESH = pl.DeviceIdType.MESH
LANES = 128


def split_rows(rows):
    first = max(32, rows * 9 // 16 // 32 * 32)
    return first, rows - first, first // 2, (rows - first) // 2


def layer_kernel(
    features, tok_hbm, gw_hbm, cot_hbm, kv_out, ig_out, u_out,
    tok, w, u, cot, cots, kvp, kvx, sq, sq_in, inv, rs, rs_in,
    ra_opp, rb_z, rb_opp, ra_x, rb_x, ra_z, send_sem, recv_sem, local_sem,
):
    rows, cols = gw_hbm.shape
    toks = tok_hbm.shape[0]
    RA, RB, HA, HB = split_rows(rows)
    r = lax.axis_index("replica")
    me = lax.axis_index("fsdp")
    zh = lax.div(me, 8)
    x = lax.rem(lax.div(me, 2), 4)
    c = lax.rem(me, 2)

    def at(plane, col, core):
        return (r, plane * 8 + col * 2 + core)

    right = at(zh, lax.rem(x + 1, 4), c)
    left = at(zh, lax.rem(x + 3, 4), c)
    partner = at(1 - zh, x, c)
    sibling = at(zh, x, 1 - c)

    def slot(plane, dx):
        return (zh if plane == 0 else 1 - zh) * 4 + lax.rem(x + dx + 4, 4)

    barrier = pltpu.get_barrier_semaphore()
    for other in (right, left, partner, sibling):
        pl.semaphore_signal(barrier, inc=1, device_id=other, device_id_type=MESH)
    pl.semaphore_wait(barrier, 4)

    sent = {}

    def send(name, src, dst, to):
        i = len(sent)
        copy = pltpu.make_async_remote_copy(
            src_ref=src, dst_ref=dst, send_sem=send_sem.at[i], recv_sem=recv_sem.at[i],
            device_id=to, device_id_type=MESH,
        )
        copy.start()
        sent[name] = copy

    def got(*names):
        for name in names:
            sent[name].wait_recv()

    a_rows, b_rows = pl.ds(0, RA), pl.ds(RA, RB)
    a_first, a_last = pl.ds(0, HA), pl.ds(HA, RA - HA)
    b_first, b_last = pl.ds(RA, HB), pl.ds(RA + HB, RB - HB)

    own = slot(0, 0)
    send("g_right_b", gw_hbm.at[b_rows], w.at[own, b_rows], right)
    send("g_left_b", gw_hbm.at[b_rows], w.at[own, b_rows], left)
    send("g_z_a", gw_hbm.at[a_rows], w.at[own, a_rows], partner)
    send("g_right_a", gw_hbm.at[a_rows], w.at[own, a_rows], right)
    send("g_left_a", gw_hbm.at[a_rows], w.at[own, a_rows], left)
    send("g_z_b", gw_hbm.at[b_rows], w.at[own, b_rows], partner)

    def columns(k, core):
        return pl.ds(pl.multiple_of((2 * k + core) * rows, rows), rows)

    blocks = features // rows // 2
    loads = []
    for k in range(blocks):
        load = pltpu.make_async_copy(tok_hbm.at[:, columns(k, c)], tok.at[0, k], local_sem.at[k])
        load.start()
        loads.append(load)
        send(f"t{k}", tok_hbm.at[:, columns(k, 1 - c)], tok.at[1, k], sibling)
    load_cot = pltpu.make_async_copy(cot_hbm, cot.at[0], local_sem.at[blocks])
    load_cot.start()
    send("cot", cot_hbm, cot.at[1], sibling)
    load_w = pltpu.make_async_copy(gw_hbm, w.at[own], local_sem.at[blocks + 1])
    load_w.start()

    RT = min(64, toks)
    lanes = min(LANES, rows)

    def square_block(half, k, fresh):
        @pl.loop(0, toks // RT)
        def _(i):
            at_rows = pl.ds(pl.multiple_of(i * RT, RT), RT)
            piece = tok[half, k, at_rows, :].astype(f32)
            piece = piece * piece
            total = piece[:, :lanes]
            for j in range(1, rows // lanes):
                total = total + piece[:, j * lanes : (j + 1) * lanes]
            if fresh:
                sq[half, at_rows, :] = total
            else:
                sq[half, at_rows, :] += total

    for half in range(2):
        for k in range(blocks):
            if half == 0:
                loads[k].wait()
            else:
                got(f"t{k}")
            square_block(half, k, k == 0)
    send("sq", sq, sq_in, sibling)
    load_cot.wait()
    got("cot", "sq")

    def wide(column, width):
        return jnp.concatenate([column] * (width // lanes), axis=1) if width > lanes else column[:, :width]

    for half in range(2):
        @pl.loop(0, toks // RT)
        def _(i):
            at_rows = pl.ds(pl.multiple_of(i * RT, RT), RT)
            total = sq[half, at_rows, :] + sq_in[1 - half, at_rows, :]
            mean = jnp.sum(total, axis=1, keepdims=True) / features
            root = jnp.broadcast_to(lax.rsqrt(mean + epsilon), (RT, lanes))
            inv[half, at_rows, :] = root
            cots[half, at_rows, :] = (cot[half, at_rows, :].astype(f32) * wide(root, cols)).astype(bf16)

    FT = min(256, rows)
    TT = min(256, toks)

    def u_block(k):
        @pl.loop(0, rows // FT)
        def _(j):
            at_rows = pl.ds(pl.multiple_of(j * FT, FT), FT)
            total = None
            for half in range(2):
                term = lax.dot_general(
                    tok[half, k, :, at_rows], cots[half], (((0,), (0,)), ((), ())),
                    preferred_element_type=f32,
                )
                total = term if total is None else total + term
            u[k, at_rows, :] = total.astype(bf16)

    def kv_block(k, fresh=False):
        for half in range(2):
            @pl.loop(0, toks // TT)
            def _(j):
                at_rows = pl.ds(pl.multiple_of(j * TT, TT), TT)
                term = jnp.dot(tok[half, k, at_rows, :], w[k], preferred_element_type=f32)
                if fresh:
                    kvp[half, at_rows, :] = term
                else:
                    kvp[half, at_rows, :] += term

    def back_block(k):
        for half in range(2):
            @pl.loop(0, toks // TT)
            def _(j):
                at_rows = pl.ds(pl.multiple_of(j * TT, TT), TT)
                weighted = lax.dot_general(
                    cot[half, at_rows, :], w[k], (((1,), (1,)), ((), ())),
                    preferred_element_type=f32,
                )
                grad = weighted * wide(inv[half, at_rows, :], rows) - tok[
                    half, k, at_rows, :
                ].astype(f32) * wide(sq[half, at_rows, :], rows)
                tok[half, k, at_rows, :] = grad.astype(bf16)

    ig_base = 64

    def ig_store(k):
        return pltpu.make_async_copy(
            tok.at[0, k], ig_out.at[:, columns(k, c)], local_sem.at[blocks + 2 + k]
        )

    def ig_send(k):
        return pltpu.make_async_remote_copy(
            src_ref=tok.at[1, k], dst_ref=ig_out.at[:, columns(k, c)],
            send_sem=send_sem.at[ig_base + k], recv_sem=recv_sem.at[ig_base + k],
            device_id=sibling, device_id_type=MESH,
        )

    def back_loop(lo, hi):
        @pl.loop(lo, hi)
        def _(k):
            back_block(k)
            ig_store(k).start()
            ig_send(k).start()

    AT = 16

    def add_rows(count, dst, dst_at, *srcs):
        @pl.loop(0, count // AT)
        def _(i):
            to = pl.ds(pl.multiple_of(dst_at + i * AT, AT), AT)
            total = u[dst, to, :].astype(f32)
            for ref, index in srcs:
                total = total + ref[(*index, pl.ds(pl.multiple_of(i * AT, AT), AT), slice(None))].astype(f32)
            u[dst, to, :] = total.astype(bf16)

    def reduce_a(plane):
        got(f"ro_r{plane}", f"ro_l{plane}")
        to_right, to_left = slot(plane, 1), slot(plane, -1)
        add_rows(HA, to_right, 0, (ra_opp, (0, plane)))
        send(f"ra_r{plane}", u.at[to_right, a_rows], ra_x.at[0, plane], right)
        add_rows(RA - HA, to_left, HA, (ra_opp, (1, plane)))
        send(f"ra_l{plane}", u.at[to_left, a_rows], ra_x.at[1, plane], left)

    def reduce_b_opposite():
        got("rz0")
        add_rows(RB, mine_o, RA, (rb_z, (0,)))
        send("rbo_r", u.at[mine_o, b_first], rb_opp.at[0, pl.ds(0, HB)], right)
        send("rbo_l", u.at[mine_o, b_last], rb_opp.at[1, pl.ds(0, RB - HB)], left)
        got("rz1")
        add_rows(RB, mine_r, RA, (rb_z, (1,)))
        got("rz2")
        add_rows(RB, mine_l, RA, (rb_z, (2,)))

    def reduce_b_side():
        got("rbo_r", "rbo_l")
        add_rows(HB, mine_r, RA, (rb_opp, (0,)))
        send("rb_r", u.at[mine_r, b_rows], rb_x.at[0], right)
        add_rows(RB - HB, mine_l, RA + HB, (rb_opp, (1,)))
        send("rb_l", u.at[mine_l, b_rows], rb_x.at[1], left)

    def u_loop(lo, hi):
        @pl.loop(lo, hi)
        def _(k):
            u_block(k)

    mine_r, mine_l, mine_o = slot(0, 1), slot(0, -1), slot(0, 2)
    far, far_r, far_l, far_o = slot(1, 0), slot(1, 1), slot(1, -1), slot(1, 2)
    got("g_right_b", "g_left_b", "g_z_a")
    send("g2_right_b", w.at[mine_l, b_first], w.at[mine_l, b_first], right)
    send("g2_left_b", w.at[mine_r, b_last], w.at[mine_r, b_last], left)
    send("gz_l", w.at[mine_l, b_rows], w.at[mine_l, b_rows], partner)
    send("gz_r", w.at[mine_r, b_rows], w.at[mine_r, b_rows], partner)
    send("h_right_a", w.at[far, a_rows], w.at[far, a_rows], right)
    send("h_left_a", w.at[far, a_rows], w.at[far, a_rows], left)
    u_loop(0, 3)
    got("g_right_a", "g_left_a")
    send("g2_right_a", w.at[mine_l, a_first], w.at[mine_l, a_first], right)
    send("g2_left_a", w.at[mine_r, a_last], w.at[mine_r, a_last], left)
    u_loop(3, 6)
    got("g2_right_b", "g2_left_b")
    send("gz_o", w.at[mine_o, b_rows], w.at[mine_o, b_rows], partner)
    u_loop(6, 8)
    for j, dx in enumerate((2, 1, -1, 0)):
        send(f"rz{j}", u.at[slot(1, dx), b_rows], rb_z.at[j], partner)
    load_w.wait()
    kv_block(own, True)

    @pl.loop(0, 2)
    def _(i):
        kv_block(zh * 4 + lax.rem(x + 1 + 2 * i, 4))

    got("h_right_a", "h_left_a")
    send("h2_right_a", w.at[far_l, a_first], w.at[far_l, a_first], right)
    send("h2_left_a", w.at[far_r, a_last], w.at[far_r, a_last], left)
    for plane in (1, 0):
        opp = slot(plane, 2)
        send(f"ro_r{plane}", u.at[opp, a_first], ra_opp.at[0, plane, pl.ds(0, HA)], right)
        send(f"ro_l{plane}", u.at[opp, a_last], ra_opp.at[1, plane, pl.ds(0, RA - HA)], left)
    got("g2_right_a", "g2_left_a", "g_z_b")
    kv_block(mine_o)
    kv_block(far)
    got("gz_l", "gz_r", "h2_right_a", "h2_left_a", "gz_o")

    @pl.loop(1, 4)
    def _(i):
        kv_block((1 - zh) * 4 + lax.rem(x + i, 4))

    send("kv", kvp.at[1], kvx, sibling)
    for half in range(2):
        @pl.loop(0, toks // RT)
        def _(i):
            at_rows = pl.ds(pl.multiple_of(i * RT, RT), RT)
            piece = kvp[half, at_rows, :] * cot[half, at_rows, :].astype(f32)
            total = piece[:, :lanes]
            for j in range(1, cols // lanes):
                total = total + piece[:, j * lanes : (j + 1) * lanes]
            rs[half, at_rows, :] = total

    send("rs", rs, rs_in, sibling)
    reduce_a(1)
    sent["sq"].wait_send()
    got("rs", "kv")
    for half in range(2):
        @pl.loop(0, toks // RT)
        def _(i):
            at_rows = pl.ds(pl.multiple_of(i * RT, RT), RT)
            scale = inv[half, at_rows, :]
            total = jnp.sum(rs[half, at_rows, :] + rs_in[1 - half, at_rows, :], axis=1, keepdims=True)
            sq[half, at_rows, :] = (jnp.broadcast_to(total, (RT, lanes)) * scale / features) * scale * scale
            if half == 0:
                whole = kvp[0, at_rows, :] + kvx[at_rows, :]
                cots[0, at_rows, :] = (whole * wide(scale, cols)).astype(bf16)

    store_kv = pltpu.make_async_copy(cots.at[0], kv_out, local_sem.at[2 * blocks + 2])
    store_kv.start()

    back_loop(0, 2)
    reduce_b_opposite()
    reduce_a(0)
    back_loop(2, 5)
    reduce_b_side()
    back_loop(5, 8)
    got("ra_r1", "ra_l1")
    add_rows(RA, far, 0, (ra_x, (0, 1)), (ra_x, (1, 1)))
    send("za", u.at[far, a_rows], ra_z, partner)
    got("rz3")
    add_rows(RB, own, RA, (rb_z, (3,)))

    store_kv.wait()

    def last_sum(lo, count, *srcs):
        @pl.loop(0, count // AT)
        def _(i):
            to = pl.ds(pl.multiple_of(lo + i * AT, AT), AT)
            total = u[own, to, :].astype(f32)
            for ref, index in srcs:
                total = total + ref[(*index, pl.ds(pl.multiple_of(i * AT, AT), AT), slice(None))].astype(f32)
            kvx[to, :] = total
        store = pltpu.make_async_copy(
            kvx.at[pl.ds(lo, count)], u_out.at[pl.ds(lo, count)], local_sem.at[2 * blocks + 3 + (lo > 0)]
        )
        store.start()
        return store

    got("rb_r", "rb_l")
    last_b = last_sum(RA, RB, (rb_x, (0,)), (rb_x, (1,)))
    got("ra_r0", "ra_l0", "za")
    last_a = last_sum(0, RA, (ra_x, (0, 0)), (ra_x, (1, 0)), (ra_z, ()))
    for name, copy in sent.items():
        if name != "sq":
            copy.wait_send()

    @pl.loop(0, blocks)
    def _(k):
        ig_store(k).wait()
        ig_send(k).wait()

    last_b.wait()
    last_a.wait()


def layer(tokens, gained, cotangent):
    toks, features = tokens.shape
    rows, cols = gained.shape
    blocks = features // rows // 2
    RA, RB, HA, HB = split_rows(rows)
    lanes = min(LANES, rows)
    any_space = pl.BlockSpec(memory_space=pl.ANY)
    vector = pltpu.VMEM((2, toks, lanes), f32)
    return pl.pallas_call(
        functools.partial(layer_kernel, features),
        out_shape=(
            jax.ShapeDtypeStruct((toks, cols), bf16),
            jax.ShapeDtypeStruct((toks, features), bf16),
            jax.ShapeDtypeStruct((rows, cols), f32),
        ),
        in_specs=[any_space] * 3,
        out_specs=(any_space,) * 3,
        scratch_shapes=[
            pltpu.VMEM((2, blocks, toks, rows), bf16),
            pltpu.VMEM((blocks, rows, cols), bf16),
            pltpu.VMEM((blocks, rows, cols), bf16),
            pltpu.VMEM((2, toks, cols), bf16),
            pltpu.VMEM((2, toks, cols), bf16),
            pltpu.VMEM((2, toks, cols), f32),
            pltpu.VMEM((toks, cols), f32),
            vector, vector, vector, vector, vector,
            pltpu.VMEM((2, 2, max(HA, RA - HA), cols), bf16),
            pltpu.VMEM((4, RB, cols), bf16),
            pltpu.VMEM((2, max(HB, RB - HB), cols), bf16),
            pltpu.VMEM((2, 2, RA, cols), bf16),
            pltpu.VMEM((2, RB, cols), bf16),
            pltpu.VMEM((RA, cols), bf16),
            pltpu.SemaphoreType.DMA((72,)),
            pltpu.SemaphoreType.DMA((72,)),
            pltpu.SemaphoreType.DMA((32,)),
        ],
        compiler_params=pltpu.CompilerParams(
            collective_id=0, has_side_effects=True, vmem_limit_bytes=62 * 1024 * 1024
        ),
        cost_estimate=pl.CostEstimate(
            flops=6 * toks * features * cols, bytes_accessed=400 * 1024 * 1024, transcendentals=0
        ),
        name="layer",
    )(tokens, gained, cotangent)


def on_device(
    tokens, kv_weight, norm_gain, cotangent, global_params, momentum, local_params, fragment_order
):
    gain = norm_gain[0].astype(f32)[:, None]
    weight = kv_weight[0].astype(f32)
    gained = (weight * gain).astype(bf16)
    fragment_slot = fragment_order[0]
    current = lax.dynamic_index_in_dim(global_params, fragment_slot, 0, keepdims=False)
    moment_old = lax.dynamic_index_in_dim(momentum, fragment_slot, 0, keepdims=False)
    drifted = current - local_params[0]
    replicas = lax.axis_size("replica")
    summed = lax.psum(drifted.astype(bf16), "replica").astype(f32)
    keys_values, input_grad, products = layer(tokens, gained, cotangent)
    weight_share = gain * products
    gain_share = jnp.sum(weight * products, axis=1)
    averaged = summed / replicas
    moment = outer_beta * moment_old + averaged
    updated = current - outer_rate * (averaged + outer_beta * moment)
    new_params = lax.dynamic_update_index_in_dim(global_params, updated, fragment_slot, 0)
    new_momentum = lax.dynamic_update_index_in_dim(momentum, moment, fragment_slot, 0)
    return (keys_values, input_grad, weight_share[None], gain_share[None], new_params, new_momentum)


def solution(mesh):
    return jax.shard_map(
        on_device,
        mesh=mesh,
        in_specs=(
            P(("replica", "fsdp"), None),
            P("replica", "fsdp", None),
            P("replica", "fsdp"),
            P(("replica", "fsdp"), None),
            P(None, "fsdp", None),
            P(None, "fsdp", None),
            P("replica", "fsdp", None),
            P(),
        ),
        out_specs=(
            P(("replica", "fsdp"), None),
            P(("replica", "fsdp"), None),
            P("replica", "fsdp", None),
            P("replica", "fsdp"),
            P(None, "fsdp", None),
            P(None, "fsdp", None),
        ),
        check_vma=False,
    )
```

```python
import functools

import jax
import jax.numpy as jnp
from jax import lax
from jax.experimental import pallas as pl
from jax.experimental.pallas import tpu as pltpu
from jax.sharding import PartitionSpec as P

epsilon = 1e-05
outer_beta = 0.9
outer_rate = 0.7
f32 = jnp.float32
bf16 = jnp.bfloat16
MESH = pl.DeviceIdType.MESH
LANES = 128


def split_rows(rows):
    first = max(32, rows * 9 // 16 // 32 * 32)
    return first, rows - first, first // 2, (rows - first) // 2


def layer_kernel(
    features, order, gain, tok_hbm, w_hbm, cot_hbm, outer_hbm, inner_hbm,
    kv_out, ig_out, u_out, drift_out,
    tok, w, u, cot, cots, kvp, kvx, sq, sq_in, inv, rs, rs_in,
    ra_opp, rb_z, rb_opp, ra_x, rb_x, ra_z,
    outer, inner, drift, drift_in, drifts, drifts_in, send_sem, recv_sem, local_sem,
):
    rows, cols = w_hbm.shape
    toks = tok_hbm.shape[0]
    RA, RB, HA, HB = split_rows(rows)
    r = lax.axis_index("replica")
    me = lax.axis_index("fsdp")
    zh = lax.div(me, 8)
    x = lax.rem(lax.div(me, 2), 4)
    c = lax.rem(me, 2)

    def at(plane, col, core):
        return (r, plane * 8 + col * 2 + core)

    right = at(zh, lax.rem(x + 1, 4), c)
    left = at(zh, lax.rem(x + 3, 4), c)
    partner = at(1 - zh, x, c)
    sibling = at(zh, x, 1 - c)
    z_lo, y = lax.div(r, 4), lax.rem(r, 4)
    peers = (
        ((1 - z_lo) * 4 + y, me),
        (z_lo * 4 + y + 1 - 2 * lax.rem(y, 2), me),
        (z_lo * 4 + 3 - y, me),
    )

    def slot(plane, dx):
        return (zh if plane == 0 else 1 - zh) * 4 + lax.rem(x + dx + 4, 4)

    blocks = features // rows // 2

    def columns(k, core):
        return pl.ds(pl.multiple_of((2 * k + core) * rows, rows), rows)

    barrier = pltpu.get_barrier_semaphore()
    around = (right, left, partner, sibling, *peers)
    for other in around:
        pl.semaphore_signal(barrier, inc=1, device_id=other, device_id_type=MESH)
    early = 2 * blocks + 5

    def load(src, dst, i):
        copy = pltpu.make_async_copy(src, dst, local_sem.at[i])
        copy.start()
        return copy

    load_w = load(w_hbm, cots.at[0], early)
    loads = [load(tok_hbm.at[:, columns(k, c)], tok.at[0, k], k) for k in range(blocks)]
    load_cot = load(cot_hbm, cot.at[0], blocks)
    load_outer = load(outer_hbm, outer, early + 2)
    load_inner = load(inner_hbm, inner, early + 3)
    pl.semaphore_wait(barrier, len(around))

    sent = {}

    def send(name, src, dst, to):
        i = len(sent)
        copy = pltpu.make_async_remote_copy(
            src_ref=src, dst_ref=dst, send_sem=send_sem.at[i], recv_sem=recv_sem.at[i],
            device_id=to, device_id_type=MESH,
        )
        copy.start()
        sent[name] = copy

    def got(*names):
        for name in names:
            sent[name].wait_recv()

    a_rows, b_rows = pl.ds(0, RA), pl.ds(RA, RB)
    a_first, a_last = pl.ds(0, HA), pl.ds(HA, RA - HA)
    b_first, b_last = pl.ds(RA, HB), pl.ds(RA + HB, RB - HB)

    own = slot(0, 0)
    lanes = min(LANES, rows)
    AT = 16

    def wide(column, width):
        return jnp.concatenate([column] * (width // lanes), axis=1) if width > lanes else column[:, :width]

    def gained(lo, count):
        @pl.loop(0, count // AT)
        def _(i):
            to = pl.ds(pl.multiple_of(lo + i * AT, AT), AT)
            w[own, to, :] = (cots[0, to, :].astype(f32) * wide(rs[0, to, :], cols)).astype(bf16)

    rs[0, pl.ds(0, rows), :] = jnp.broadcast_to(gain[...].astype(f32), (lanes, rows)).T
    load_w.wait()
    gained(RA, RB)
    send("g_right_b", w.at[own, b_rows], w.at[own, b_rows], right)
    send("g_left_b", w.at[own, b_rows], w.at[own, b_rows], left)
    gained(0, RA)
    send("g_z_a", w.at[own, a_rows], w.at[own, a_rows], partner)
    send("g_right_a", w.at[own, a_rows], w.at[own, a_rows], right)
    send("g_left_a", w.at[own, a_rows], w.at[own, a_rows], left)
    send("g_z_b", w.at[own, b_rows], w.at[own, b_rows], partner)
    for k in range(blocks):
        send(f"t{k}", tok_hbm.at[:, columns(k, 1 - c)], tok.at[1, k], sibling)
    send("cot", cot_hbm, cot.at[1], sibling)

    load_outer.wait()
    load_inner.wait()
    drift[...] = (outer[order[0]] - inner[...]).astype(bf16)
    send("d0", drift, drift_in, peers[0])

    def drift_step(step):
        got(f"d{step}")
        if step == 0:
            drifts[0] = drift[...].astype(f32) + drift_in[...].astype(f32)
        else:
            drifts[step] = drifts[step - 1] + drifts_in[step - 1]
        if step < 2:
            send(f"d{step + 1}", drifts.at[step], drifts_in.at[step], peers[step + 1])

    RT = min(64, toks)

    def square_block(half, k, fresh):
        @pl.loop(0, toks // RT)
        def _(i):
            at_rows = pl.ds(pl.multiple_of(i * RT, RT), RT)
            piece = tok[half, k, at_rows, :].astype(f32)
            piece = piece * piece
            total = piece[:, :lanes]
            for j in range(1, rows // lanes):
                total = total + piece[:, j * lanes : (j + 1) * lanes]
            if fresh:
                sq[half, at_rows, :] = total
            else:
                sq[half, at_rows, :] += total

    for half in range(2):
        for k in range(blocks):
            if half == 0:
                loads[k].wait()
            else:
                got(f"t{k}")
            square_block(half, k, k == 0)
    send("sq", sq, sq_in, sibling)
    load_cot.wait()
    got("cot", "sq")

    for half in range(2):
        @pl.loop(0, toks // RT)
        def _(i):
            at_rows = pl.ds(pl.multiple_of(i * RT, RT), RT)
            total = sq[half, at_rows, :] + sq_in[1 - half, at_rows, :]
            mean = jnp.sum(total, axis=1, keepdims=True) / features
            root = jnp.broadcast_to(lax.rsqrt(mean + epsilon), (RT, lanes))
            inv[half, at_rows, :] = root
            cots[half, at_rows, :] = (cot[half, at_rows, :].astype(f32) * wide(root, cols)).astype(bf16)

    FT = min(256, rows)
    TT = min(256, toks)

    def u_block(k):
        @pl.loop(0, rows // FT)
        def _(j):
            at_rows = pl.ds(pl.multiple_of(j * FT, FT), FT)
            total = None
            for half in range(2):
                term = lax.dot_general(
                    tok[half, k, :, at_rows], cots[half], (((0,), (0,)), ((), ())),
                    preferred_element_type=f32,
                )
                total = term if total is None else total + term
            u[k, at_rows, :] = total.astype(bf16)

    def kv_block(k, fresh=False):
        for half in range(2):
            @pl.loop(0, toks // TT)
            def _(j):
                at_rows = pl.ds(pl.multiple_of(j * TT, TT), TT)
                term = jnp.dot(tok[half, k, at_rows, :], w[k], preferred_element_type=f32)
                if fresh:
                    kvp[half, at_rows, :] = term
                else:
                    kvp[half, at_rows, :] += term

    def back_block(k):
        for half in range(2):
            @pl.loop(0, toks // TT)
            def _(j):
                at_rows = pl.ds(pl.multiple_of(j * TT, TT), TT)
                weighted = lax.dot_general(
                    cot[half, at_rows, :], w[k], (((1,), (1,)), ((), ())),
                    preferred_element_type=f32,
                )
                grad = weighted * wide(inv[half, at_rows, :], rows) - tok[
                    half, k, at_rows, :
                ].astype(f32) * wide(sq[half, at_rows, :], rows)
                tok[half, k, at_rows, :] = grad.astype(bf16)

    ig_base = 64

    def ig_store(k):
        return pltpu.make_async_copy(
            tok.at[0, k], ig_out.at[:, columns(k, c)], local_sem.at[blocks + 2 + k]
        )

    def ig_send(k):
        return pltpu.make_async_remote_copy(
            src_ref=tok.at[1, k], dst_ref=ig_out.at[:, columns(k, c)],
            send_sem=send_sem.at[ig_base + k], recv_sem=recv_sem.at[ig_base + k],
            device_id=sibling, device_id_type=MESH,
        )

    def back_loop(lo, hi):
        @pl.loop(lo, hi)
        def _(k):
            back_block(k)
            ig_store(k).start()
            ig_send(k).start()

    def add_rows(count, dst, dst_at, *srcs):
        @pl.loop(0, count // AT)
        def _(i):
            to = pl.ds(pl.multiple_of(dst_at + i * AT, AT), AT)
            total = u[dst, to, :].astype(f32)
            for ref, index in srcs:
                total = total + ref[(*index, pl.ds(pl.multiple_of(i * AT, AT), AT), slice(None))].astype(f32)
            u[dst, to, :] = total.astype(bf16)

    def reduce_a(plane):
        got(f"ro_r{plane}", f"ro_l{plane}")
        to_right, to_left = slot(plane, 1), slot(plane, -1)
        add_rows(HA, to_right, 0, (ra_opp, (0, plane)))
        send(f"ra_r{plane}", u.at[to_right, a_rows], ra_x.at[0, plane], right)
        add_rows(RA - HA, to_left, HA, (ra_opp, (1, plane)))
        send(f"ra_l{plane}", u.at[to_left, a_rows], ra_x.at[1, plane], left)

    def reduce_b_opposite():
        got("rz0")
        add_rows(RB, mine_o, RA, (rb_z, (0,)))
        send("rbo_r", u.at[mine_o, b_first], rb_opp.at[0, pl.ds(0, HB)], right)
        send("rbo_l", u.at[mine_o, b_last], rb_opp.at[1, pl.ds(0, RB - HB)], left)
        got("rz1")
        add_rows(RB, mine_r, RA, (rb_z, (1,)))
        got("rz2")
        add_rows(RB, mine_l, RA, (rb_z, (2,)))

    def reduce_b_side():
        got("rbo_r", "rbo_l")
        add_rows(HB, mine_r, RA, (rb_opp, (0,)))
        send("rb_r", u.at[mine_r, b_rows], rb_x.at[0], right)
        add_rows(RB - HB, mine_l, RA + HB, (rb_opp, (1,)))
        send("rb_l", u.at[mine_l, b_rows], rb_x.at[1], left)

    def u_loop(lo, hi):
        @pl.loop(lo, hi)
        def _(k):
            u_block(k)

    mine_r, mine_l, mine_o = slot(0, 1), slot(0, -1), slot(0, 2)
    far, far_r, far_l, far_o = slot(1, 0), slot(1, 1), slot(1, -1), slot(1, 2)
    got("g_right_b", "g_left_b", "g_z_a")
    send("g2_right_b", w.at[mine_l, b_first], w.at[mine_l, b_first], right)
    send("g2_left_b", w.at[mine_r, b_last], w.at[mine_r, b_last], left)
    send("gz_l", w.at[mine_l, b_rows], w.at[mine_l, b_rows], partner)
    send("gz_r", w.at[mine_r, b_rows], w.at[mine_r, b_rows], partner)
    send("h_right_a", w.at[far, a_rows], w.at[far, a_rows], right)
    send("h_left_a", w.at[far, a_rows], w.at[far, a_rows], left)
    u_loop(0, 3)
    drift_step(0)
    got("g_right_a", "g_left_a")
    send("g2_right_a", w.at[mine_l, a_first], w.at[mine_l, a_first], right)
    send("g2_left_a", w.at[mine_r, a_last], w.at[mine_r, a_last], left)
    u_loop(3, 6)
    drift_step(1)
    got("g2_right_b", "g2_left_b")
    send("gz_o", w.at[mine_o, b_rows], w.at[mine_o, b_rows], partner)
    u_loop(6, 8)
    for j, dx in enumerate((2, 1, -1, 0)):
        send(f"rz{j}", u.at[slot(1, dx), b_rows], rb_z.at[j], partner)
    kv_block(own, True)
    drift_step(2)
    store_drift = load(drifts.at[2], drift_out, early)

    @pl.loop(0, 2)
    def _(i):
        kv_block(zh * 4 + lax.rem(x + 1 + 2 * i, 4))

    got("h_right_a", "h_left_a")
    send("h2_right_a", w.at[far_l, a_first], w.at[far_l, a_first], right)
    send("h2_left_a", w.at[far_r, a_last], w.at[far_r, a_last], left)
    for plane in (1, 0):
        opp = slot(plane, 2)
        send(f"ro_r{plane}", u.at[opp, a_first], ra_opp.at[0, plane, pl.ds(0, HA)], right)
        send(f"ro_l{plane}", u.at[opp, a_last], ra_opp.at[1, plane, pl.ds(0, RA - HA)], left)
    got("g2_right_a", "g2_left_a", "g_z_b")
    kv_block(mine_o)
    kv_block(far)
    got("gz_l", "gz_r", "h2_right_a", "h2_left_a", "gz_o")

    @pl.loop(1, 4)
    def _(i):
        kv_block((1 - zh) * 4 + lax.rem(x + i, 4))

    send("kv", kvp.at[1], kvx, sibling)
    for half in range(2):
        @pl.loop(0, toks // RT)
        def _(i):
            at_rows = pl.ds(pl.multiple_of(i * RT, RT), RT)
            piece = kvp[half, at_rows, :] * cot[half, at_rows, :].astype(f32)
            total = piece[:, :lanes]
            for j in range(1, cols // lanes):
                total = total + piece[:, j * lanes : (j + 1) * lanes]
            rs[half, at_rows, :] = total

    send("rs", rs, rs_in, sibling)
    reduce_a(1)
    sent["sq"].wait_send()
    got("rs", "kv")
    for half in range(2):
        @pl.loop(0, toks // RT)
        def _(i):
            at_rows = pl.ds(pl.multiple_of(i * RT, RT), RT)
            scale = inv[half, at_rows, :]
            total = jnp.sum(rs[half, at_rows, :] + rs_in[1 - half, at_rows, :], axis=1, keepdims=True)
            sq[half, at_rows, :] = (jnp.broadcast_to(total, (RT, lanes)) * scale / features) * scale * scale
            if half == 0:
                whole = kvp[0, at_rows, :] + kvx[at_rows, :]
                cots[0, at_rows, :] = (whole * wide(scale, cols)).astype(bf16)

    store_kv = pltpu.make_async_copy(cots.at[0], kv_out, local_sem.at[2 * blocks + 2])
    store_kv.start()

    back_loop(0, 2)
    reduce_b_opposite()
    reduce_a(0)
    back_loop(2, 5)
    reduce_b_side()
    back_loop(5, 8)
    got("ra_r1", "ra_l1")
    add_rows(RA, far, 0, (ra_x, (0, 1)), (ra_x, (1, 1)))
    send("za", u.at[far, a_rows], ra_z, partner)
    got("rz3")
    add_rows(RB, own, RA, (rb_z, (3,)))

    store_kv.wait()

    def last_sum(lo, count, *srcs):
        @pl.loop(0, count // AT)
        def _(i):
            to = pl.ds(pl.multiple_of(lo + i * AT, AT), AT)
            total = u[own, to, :].astype(f32)
            for ref, index in srcs:
                total = total + ref[(*index, pl.ds(pl.multiple_of(i * AT, AT), AT), slice(None))].astype(f32)
            kvx[to, :] = total
        store = pltpu.make_async_copy(
            kvx.at[pl.ds(lo, count)], u_out.at[pl.ds(lo, count)], local_sem.at[2 * blocks + 3 + (lo > 0)]
        )
        store.start()
        return store

    got("rb_r", "rb_l")
    last_b = last_sum(RA, RB, (rb_x, (0,)), (rb_x, (1,)))
    got("ra_r0", "ra_l0", "za")
    last_a = last_sum(0, RA, (ra_x, (0, 0)), (ra_x, (1, 0)), (ra_z, ()))
    for name, copy in sent.items():
        if name != "sq":
            copy.wait_send()

    @pl.loop(0, blocks)
    def _(k):
        ig_store(k).wait()
        ig_send(k).wait()

    store_drift.wait()
    last_b.wait()
    last_a.wait()


def layer(tokens, weight, gain, cotangent, outer, inner, order):
    toks, features = tokens.shape
    rows, cols = weight.shape
    blocks = features // rows // 2
    RA, RB, HA, HB = split_rows(rows)
    lanes = min(LANES, rows)
    any_space = pl.BlockSpec(memory_space=pl.ANY)
    vector = pltpu.VMEM((2, toks, lanes), f32)
    return pl.pallas_call(
        functools.partial(layer_kernel, features),
        out_shape=(
            jax.ShapeDtypeStruct((toks, cols), bf16),
            jax.ShapeDtypeStruct((toks, features), bf16),
            jax.ShapeDtypeStruct((rows, cols), f32),
            jax.ShapeDtypeStruct(inner.shape, f32),
        ),
        in_specs=[pl.BlockSpec(memory_space=pltpu.SMEM), pl.BlockSpec(memory_space=pltpu.VMEM)]
        + [any_space] * 5,
        out_specs=(any_space,) * 4,
        scratch_shapes=[
            pltpu.VMEM((2, blocks, toks, rows), bf16),
            pltpu.VMEM((blocks, rows, cols), bf16),
            pltpu.VMEM((blocks, rows, cols), bf16),
            pltpu.VMEM((2, toks, cols), bf16),
            pltpu.VMEM((2, toks, cols), bf16),
            pltpu.VMEM((2, toks, cols), f32),
            pltpu.VMEM((toks, cols), f32),
            vector, vector, vector, vector, vector,
            pltpu.VMEM((2, 2, max(HA, RA - HA), cols), bf16),
            pltpu.VMEM((4, RB, cols), bf16),
            pltpu.VMEM((2, max(HB, RB - HB), cols), bf16),
            pltpu.VMEM((2, 2, RA, cols), bf16),
            pltpu.VMEM((2, RB, cols), bf16),
            pltpu.VMEM((RA, cols), bf16),
            pltpu.VMEM(outer.shape, f32),
            pltpu.VMEM(inner.shape, f32),
            pltpu.VMEM(inner.shape, bf16),
            pltpu.VMEM(inner.shape, bf16),
            pltpu.VMEM((3, *inner.shape), f32),
            pltpu.VMEM((2, *inner.shape), f32),
            pltpu.SemaphoreType.DMA((72,)),
            pltpu.SemaphoreType.DMA((72,)),
            pltpu.SemaphoreType.DMA((32,)),
        ],
        compiler_params=pltpu.CompilerParams(
            collective_id=0, has_side_effects=True, vmem_limit_bytes=60 * 1024 * 1024
        ),
        cost_estimate=pl.CostEstimate(
            flops=6 * toks * features * cols, bytes_accessed=400 * 1024 * 1024, transcendentals=0
        ),
        name="layer",
    )(order, gain, tokens, weight, cotangent, outer, inner)


PIECES = 8


def finish_kernel(
    replicas, order, gain, ig_in, kv_in, u_in, drift_in, w_in, outer_in, moment_in,
    kv_out, ig_out, wg_out, gg_out, outer_out, moment_out,
    ig, kv, u, w, column, partial, share, drift, outer, moment, sem,
):
    rows, cols = u.shape
    lanes = min(LANES, rows)
    started = []

    def copy(src, dst):
        move = pltpu.make_async_copy(src, dst, sem.at[len(started)])
        move.start()
        started.append(move)
        return move

    get_u, get_w = copy(u_in, u), copy(w_in, w)
    get_drift, get_outer, get_moment = copy(drift_in, drift), copy(outer_in, outer), copy(moment_in, moment)
    step = ig_in.shape[0] // PIECES
    pieces = [pl.ds(i * step, step) for i in range(PIECES)]
    gets = [copy(kv_in, kv)] + [copy(ig_in.at[p], ig.at[p]) for p in pieces]
    puts = [(kv, kv_out)] + [(ig.at[p], ig_out.at[p]) for p in pieces]
    moves = []

    def pass_on(count):
        for _ in range(count):
            gets.pop(0).wait()
            moves.append(copy(*puts.pop(0)))

    column[...] = jnp.broadcast_to(gain[...].astype(f32), (lanes, rows)).T
    get_u.wait()
    get_w.wait()
    RT = 32

    @pl.loop(0, rows // RT)
    def _(i):
        at_rows = pl.ds(pl.multiple_of(i * RT, RT), RT)
        whole = u[at_rows, :]
        product = whole * w[at_rows, :].astype(f32)
        total = product[:, :lanes]
        for j in range(1, cols // lanes):
            total = total + product[:, j * lanes : (j + 1) * lanes]
        partial[at_rows, :] = total
        u[at_rows, :] = whole * jnp.concatenate([column[at_rows, :]] * (cols // lanes), axis=1)

    moves.append(copy(u, wg_out))
    pass_on(3)
    share[...] = jnp.sum(partial[...].T, axis=0, keepdims=True)
    moves.append(copy(share, gg_out))
    pass_on(2)
    get_drift.wait()
    get_outer.wait()
    get_moment.wait()
    now = order[0]
    averaged = drift[...] / replicas
    fresh = outer_beta * moment[now] + averaged
    moment[now] = fresh
    outer[now] = outer[now] - outer_rate * (averaged + outer_beta * fresh)
    moves.append(copy(moment, moment_out))
    moves.append(copy(outer, outer_out))
    pass_on(len(gets))
    for move in moves:
        move.wait()


def finish(replicas, order, ig, kv, u, drift, weight, gain, outer, moment):
    rows, cols = u.shape
    lanes = min(LANES, rows)
    any_space = pl.BlockSpec(memory_space=pl.ANY)
    return pl.pallas_call(
        functools.partial(finish_kernel, replicas),
        out_shape=(
            jax.ShapeDtypeStruct(kv.shape, bf16),
            jax.ShapeDtypeStruct(ig.shape, bf16),
            jax.ShapeDtypeStruct(u.shape, f32),
            jax.ShapeDtypeStruct(gain.shape, f32),
            jax.ShapeDtypeStruct(outer.shape, f32),
            jax.ShapeDtypeStruct(moment.shape, f32),
        ),
        in_specs=[pl.BlockSpec(memory_space=pltpu.SMEM), pl.BlockSpec(memory_space=pltpu.VMEM)]
        + [any_space] * 7,
        out_specs=(any_space,) * 6,
        scratch_shapes=[
            pltpu.VMEM(ig.shape, bf16),
            pltpu.VMEM(kv.shape, bf16),
            pltpu.VMEM((rows, cols), f32),
            pltpu.VMEM((rows, cols), bf16),
            pltpu.VMEM((rows, lanes), f32),
            pltpu.VMEM((rows, lanes), f32),
            pltpu.VMEM(gain.shape, f32),
            pltpu.VMEM(drift.shape, f32),
            pltpu.VMEM(outer.shape, f32),
            pltpu.VMEM(moment.shape, f32),
            pltpu.SemaphoreType.DMA((32,)),
        ],
        compiler_params=pltpu.CompilerParams(vmem_limit_bytes=60 * 1024 * 1024),
        name="finish",
    )(order, gain, ig, kv, u, drift, weight, outer, moment)


def on_device(
    tokens, kv_weight, norm_gain, cotangent, global_params, momentum, local_params, fragment_order
):
    weight = kv_weight[0]
    kv, ig, u, drift = layer(
        tokens, weight, norm_gain, cotangent, global_params, local_params[0], fragment_order
    )
    keys_values, input_grad, weight_grad, gain_grad, new_params, new_momentum = finish(
        lax.axis_size("replica"), fragment_order, ig, kv, u, drift, weight, norm_gain, global_params, momentum
    )
    return (keys_values, input_grad, weight_grad[None], gain_grad, new_params, new_momentum)


def solution(mesh):
    return jax.shard_map(
        on_device,
        mesh=mesh,
        in_specs=(
            P(("replica", "fsdp"), None),
            P("replica", "fsdp", None),
            P("replica", "fsdp"),
            P(("replica", "fsdp"), None),
            P(None, "fsdp", None),
            P(None, "fsdp", None),
            P("replica", "fsdp", None),
            P(),
        ),
        out_specs=(
            P(("replica", "fsdp"), None),
            P(("replica", "fsdp"), None),
            P("replica", "fsdp", None),
            P("replica", "fsdp"),
            P(None, "fsdp", None),
            P(None, "fsdp", None),
        ),
        check_vma=False,
    )
```

```python
import functools

import jax
import jax.numpy as jnp
from jax import lax
from jax.experimental import pallas as pl
from jax.experimental.pallas import tpu as pltpu
from jax.sharding import PartitionSpec as P

epsilon = 1e-05
outer_beta = 0.9
outer_rate = 0.7
f32 = jnp.float32
bf16 = jnp.bfloat16
MESH = pl.DeviceIdType.MESH
LANES = 128


def split_rows(rows):
    first = max(32, rows * 9 // 16 // 32 * 32)
    return first, rows - first, first // 2, (rows - first) // 2


def layer_kernel(
    features, order, gain, tok_hbm, w_hbm, cot_hbm, outer_hbm, inner_hbm,
    kv_out, ig_out, own_out, xa_out, za_out, xb_out, drift_out,
    tok, w, u, cot, cots, kvp, kvx, sq, sq_in, inv, rs, rs_in,
    ra_opp, rb_z, rb_opp, ra_x,
    outer, inner, drift, drift_in, drifts, drifts_in, send_sem, recv_sem, local_sem,
):
    rows, cols = w_hbm.shape
    toks = tok_hbm.shape[0]
    RA, RB, HA, HB = split_rows(rows)
    r = lax.axis_index("replica")
    me = lax.axis_index("fsdp")
    zh = lax.div(me, 8)
    x = lax.rem(lax.div(me, 2), 4)
    c = lax.rem(me, 2)

    def at(plane, col, core):
        return (r, plane * 8 + col * 2 + core)

    right = at(zh, lax.rem(x + 1, 4), c)
    left = at(zh, lax.rem(x + 3, 4), c)
    partner = at(1 - zh, x, c)
    sibling = at(zh, x, 1 - c)
    z_lo, y = lax.div(r, 4), lax.rem(r, 4)
    peers = (
        ((1 - z_lo) * 4 + y, me),
        (z_lo * 4 + y + 1 - 2 * lax.rem(y, 2), me),
        (z_lo * 4 + 3 - y, me),
    )

    def slot(plane, dx):
        return (zh if plane == 0 else 1 - zh) * 4 + lax.rem(x + dx + 4, 4)

    blocks = features // rows // 2

    def columns(k, core):
        return pl.ds(pl.multiple_of((2 * k + core) * rows, rows), rows)

    barrier = pltpu.get_barrier_semaphore()
    around = (right, left, partner, sibling, *peers)
    for other in around:
        pl.semaphore_signal(barrier, inc=1, device_id=other, device_id_type=MESH)
    early = 2 * blocks + 5

    def load(src, dst, i):
        copy = pltpu.make_async_copy(src, dst, local_sem.at[i])
        copy.start()
        return copy

    load_w = load(w_hbm, cots.at[0], early)
    loads = [load(tok_hbm.at[:, columns(k, c)], tok.at[0, k], k) for k in range(blocks)]
    load_cot = load(cot_hbm, cot.at[0], blocks)
    load_outer = load(outer_hbm, outer, early + 2)
    load_inner = load(inner_hbm, inner, early + 3)
    pl.semaphore_wait(barrier, len(around))

    sent = {}

    def send(name, src, dst, to):
        i = len(sent)
        copy = pltpu.make_async_remote_copy(
            src_ref=src, dst_ref=dst, send_sem=send_sem.at[i], recv_sem=recv_sem.at[i],
            device_id=to, device_id_type=MESH,
        )
        copy.start()
        sent[name] = copy

    def got(*names):
        for name in names:
            sent[name].wait_recv()

    a_rows, b_rows = pl.ds(0, RA), pl.ds(RA, RB)
    a_first, a_last = pl.ds(0, HA), pl.ds(HA, RA - HA)
    b_first, b_last = pl.ds(RA, HB), pl.ds(RA + HB, RB - HB)

    own = slot(0, 0)
    lanes = min(LANES, rows)
    AT = 16

    def wide(column, width):
        return jnp.concatenate([column] * (width // lanes), axis=1) if width > lanes else column[:, :width]

    def gained(lo, count):
        @pl.loop(0, count // AT)
        def _(i):
            to = pl.ds(pl.multiple_of(lo + i * AT, AT), AT)
            w[own, to, :] = (cots[0, to, :].astype(f32) * wide(rs[0, to, :], cols)).astype(bf16)

    rs[0, pl.ds(0, rows), :] = jnp.broadcast_to(gain[...].astype(f32), (lanes, rows)).T
    load_w.wait()
    gained(RA, RB)
    send("g_right_b", w.at[own, b_rows], w.at[own, b_rows], right)
    send("g_left_b", w.at[own, b_rows], w.at[own, b_rows], left)
    gained(0, RA)
    send("g_z_a", w.at[own, a_rows], w.at[own, a_rows], partner)
    send("g_right_a", w.at[own, a_rows], w.at[own, a_rows], right)
    send("g_left_a", w.at[own, a_rows], w.at[own, a_rows], left)
    send("g_z_b", w.at[own, b_rows], w.at[own, b_rows], partner)
    for k in range(blocks):
        send(f"t{k}", tok_hbm.at[:, columns(k, 1 - c)], tok.at[1, k], sibling)
    send("cot", cot_hbm, cot.at[1], sibling)

    load_outer.wait()
    load_inner.wait()
    drift[...] = (outer[order[0]] - inner[...]).astype(bf16)
    n_half, n_quarter = drift.shape[0] // 2, drift.shape[0] // 4
    keep = lax.rem(y + lax.div(y, 2), 2)
    upper = lax.div(y, 2)
    half_at = pl.multiple_of(keep * n_half, n_half)
    quarter_at = pl.multiple_of(half_at + upper * n_quarter, n_quarter)
    my_half, my_quarter = pl.ds(half_at, n_half), pl.ds(quarter_at, n_quarter)
    other_half = pl.ds(pl.multiple_of((1 - keep) * n_half, n_half), n_half)
    other_quarter = pl.ds(pl.multiple_of(half_at + (1 - upper) * n_quarter, n_quarter), n_quarter)
    send("d0", drift.at[other_half], drift_in.at[pl.ds(0, n_half)], peers[1])

    def drift_step(step):
        got(f"d{step}")
        if step == 0:
            mine_in = pl.ds(pl.multiple_of(upper * n_quarter, n_quarter), n_quarter)
            other_in = pl.ds(pl.multiple_of((1 - upper) * n_quarter, n_quarter), n_quarter)
            drifts[my_quarter, :] = drift[my_quarter, :].astype(f32) + drift_in[mine_in, :].astype(f32)
            drifts_in[0] = drift[other_quarter, :].astype(f32) + drift_in[other_in, :].astype(f32)
            send("d1", drifts_in.at[0], drifts_in.at[1], peers[2])
        elif step == 1:
            total = (drifts[my_quarter, :] + drifts_in[1]).astype(bf16)
            drift_in[pl.ds(n_half, n_quarter), :] = total
            send("d2", drift_in.at[pl.ds(n_half, n_quarter)], drift_in.at[pl.ds(n_half + n_quarter, n_quarter)], peers[0])
        elif step == 2:
            drifts[my_quarter, :] = (
                drift_in[pl.ds(n_half, n_quarter), :].astype(f32)
                + drift_in[pl.ds(n_half + n_quarter, n_quarter), :].astype(f32)
            )
            send("d3", drifts.at[my_quarter], drifts.at[my_quarter], peers[2])
        elif step == 3:
            send("d4", drifts.at[my_half], drifts.at[my_half], peers[1])

    RT = min(64, toks)

    def square_block(half, k, fresh):
        @pl.loop(0, toks // RT)
        def _(i):
            at_rows = pl.ds(pl.multiple_of(i * RT, RT), RT)
            piece = tok[half, k, at_rows, :].astype(f32)
            piece = piece * piece
            total = piece[:, :lanes]
            for j in range(1, rows // lanes):
                total = total + piece[:, j * lanes : (j + 1) * lanes]
            if fresh:
                sq[half, at_rows, :] = total
            else:
                sq[half, at_rows, :] += total

    for half in range(2):
        for k in range(blocks):
            if half == 0:
                loads[k].wait()
            else:
                got(f"t{k}")
            square_block(half, k, k == 0)
    send("sq", sq, sq_in, sibling)
    load_cot.wait()
    got("cot", "sq")

    for half in range(2):
        @pl.loop(0, toks // RT)
        def _(i):
            at_rows = pl.ds(pl.multiple_of(i * RT, RT), RT)
            total = sq[half, at_rows, :] + sq_in[1 - half, at_rows, :]
            mean = jnp.sum(total, axis=1, keepdims=True) / features
            root = jnp.broadcast_to(lax.rsqrt(mean + epsilon), (RT, lanes))
            inv[half, at_rows, :] = root
            cots[half, at_rows, :] = (cot[half, at_rows, :].astype(f32) * wide(root, cols)).astype(bf16)

    FT = min(256, rows)
    TT = min(256, toks)

    def u_block(k):
        @pl.loop(0, rows // FT)
        def _(j):
            at_rows = pl.ds(pl.multiple_of(j * FT, FT), FT)
            total = None
            for half in range(2):
                term = lax.dot_general(
                    tok[half, k, :, at_rows], cots[half], (((0,), (0,)), ((), ())),
                    preferred_element_type=f32,
                )
                total = term if total is None else total + term
            u[k, at_rows, :] = total.astype(bf16)

    def kv_block(k, fresh=False):
        for half in range(2):
            @pl.loop(0, toks // TT)
            def _(j):
                at_rows = pl.ds(pl.multiple_of(j * TT, TT), TT)
                term = jnp.dot(tok[half, k, at_rows, :], w[k], preferred_element_type=f32)
                if fresh:
                    kvp[half, at_rows, :] = term
                else:
                    kvp[half, at_rows, :] += term

    def back_block(k):
        for half in range(2):
            @pl.loop(0, toks // TT)
            def _(j):
                at_rows = pl.ds(pl.multiple_of(j * TT, TT), TT)
                weighted = lax.dot_general(
                    cot[half, at_rows, :], w[k], (((1,), (1,)), ((), ())),
                    preferred_element_type=f32,
                )
                grad = weighted * wide(inv[half, at_rows, :], rows) - tok[
                    half, k, at_rows, :
                ].astype(f32) * wide(sq[half, at_rows, :], rows)
                tok[half, k, at_rows, :] = grad.astype(bf16)

    ig_base = 64

    def ig_store(k):
        return pltpu.make_async_copy(
            tok.at[0, k], ig_out.at[:, columns(k, c)], local_sem.at[blocks + 2 + k]
        )

    def ig_send(k):
        return pltpu.make_async_remote_copy(
            src_ref=tok.at[1, k], dst_ref=ig_out.at[:, columns(k, c)],
            send_sem=send_sem.at[ig_base + k], recv_sem=recv_sem.at[ig_base + k],
            device_id=sibling, device_id_type=MESH,
        )

    def back_loop(lo, hi):
        @pl.loop(lo, hi)
        def _(k):
            back_block(k)
            ig_store(k).start()
            ig_send(k).start()

    def add_rows(count, dst, dst_at, *srcs):
        @pl.loop(0, count // AT)
        def _(i):
            to = pl.ds(pl.multiple_of(dst_at + i * AT, AT), AT)
            total = u[dst, to, :].astype(f32)
            for ref, index in srcs:
                total = total + ref[(*index, pl.ds(pl.multiple_of(i * AT, AT), AT), slice(None))].astype(f32)
            u[dst, to, :] = total.astype(bf16)

    def reduce_a(plane):
        got(f"ro_r{plane}", f"ro_l{plane}")
        to_right, to_left = slot(plane, 1), slot(plane, -1)
        add_rows(HA, to_right, 0, (ra_opp, (0, plane)))
        land = xa_out if plane == 0 else ra_x
        send(f"ra_r{plane}", u.at[to_right, a_rows], land.at[0], right)
        add_rows(RA - HA, to_left, HA, (ra_opp, (1, plane)))
        send(f"ra_l{plane}", u.at[to_left, a_rows], land.at[1], left)

    def reduce_b_opposite():
        got("rz0")
        add_rows(RB, mine_o, RA, (rb_z, (0,)))
        send("rbo_r", u.at[mine_o, b_first], rb_opp.at[0, pl.ds(0, HB)], right)
        send("rbo_l", u.at[mine_o, b_last], rb_opp.at[1, pl.ds(0, RB - HB)], left)
        got("rz1")
        add_rows(RB, mine_r, RA, (rb_z, (1,)))
        got("rz2")
        add_rows(RB, mine_l, RA, (rb_z, (2,)))

    def reduce_b_side():
        got("rbo_r", "rbo_l")
        add_rows(HB, mine_r, RA, (rb_opp, (0,)))
        send("rb_r", u.at[mine_r, b_rows], xb_out.at[0], right)
        add_rows(RB - HB, mine_l, RA + HB, (rb_opp, (1,)))
        send("rb_l", u.at[mine_l, b_rows], xb_out.at[1], left)

    def u_loop(lo, hi):
        @pl.loop(lo, hi)
        def _(k):
            u_block(k)

    mine_r, mine_l, mine_o = slot(0, 1), slot(0, -1), slot(0, 2)
    far, far_r, far_l, far_o = slot(1, 0), slot(1, 1), slot(1, -1), slot(1, 2)
    got("g_right_b", "g_left_b", "g_z_a")
    send("g2_right_b", w.at[mine_l, b_first], w.at[mine_l, b_first], right)
    send("g2_left_b", w.at[mine_r, b_last], w.at[mine_r, b_last], left)
    send("gz_l", w.at[mine_l, b_rows], w.at[mine_l, b_rows], partner)
    send("gz_r", w.at[mine_r, b_rows], w.at[mine_r, b_rows], partner)
    send("h_right_a", w.at[far, a_rows], w.at[far, a_rows], right)
    send("h_left_a", w.at[far, a_rows], w.at[far, a_rows], left)
    u_loop(0, 3)
    drift_step(0)
    got("g_right_a", "g_left_a")
    send("g2_right_a", w.at[mine_l, a_first], w.at[mine_l, a_first], right)
    send("g2_left_a", w.at[mine_r, a_last], w.at[mine_r, a_last], left)
    u_loop(3, 6)
    drift_step(1)
    got("g2_right_b", "g2_left_b")
    send("gz_o", w.at[mine_o, b_rows], w.at[mine_o, b_rows], partner)
    u_loop(6, 8)
    for j, dx in enumerate((2, 1, -1, 0)):
        send(f"rz{j}", u.at[slot(1, dx), b_rows], rb_z.at[j], partner)
    kv_block(own, True)
    drift_step(2)

    @pl.loop(0, 2)
    def _(i):
        kv_block(zh * 4 + lax.rem(x + 1 + 2 * i, 4))

    got("h_right_a", "h_left_a")
    send("h2_right_a", w.at[far_l, a_first], w.at[far_l, a_first], right)
    send("h2_left_a", w.at[far_r, a_last], w.at[far_r, a_last], left)
    for plane in (1, 0):
        opp = slot(plane, 2)
        send(f"ro_r{plane}", u.at[opp, a_first], ra_opp.at[0, plane, pl.ds(0, HA)], right)
        send(f"ro_l{plane}", u.at[opp, a_last], ra_opp.at[1, plane, pl.ds(0, RA - HA)], left)
    drift_step(3)
    got("g2_right_a", "g2_left_a", "g_z_b")
    kv_block(mine_o)
    kv_block(far)
    got("gz_l", "gz_r", "h2_right_a", "h2_left_a", "gz_o")

    @pl.loop(1, 4)
    def _(i):
        kv_block((1 - zh) * 4 + lax.rem(x + i, 4))

    send("kv", kvp.at[1], kvx, sibling)
    for half in range(2):
        @pl.loop(0, toks // RT)
        def _(i):
            at_rows = pl.ds(pl.multiple_of(i * RT, RT), RT)
            piece = kvp[half, at_rows, :] * cot[half, at_rows, :].astype(f32)
            total = piece[:, :lanes]
            for j in range(1, cols // lanes):
                total = total + piece[:, j * lanes : (j + 1) * lanes]
            rs[half, at_rows, :] = total

    send("rs", rs, rs_in, sibling)
    got("d4")
    store_drift = load(drifts, drift_out, early)
    reduce_a(1)
    sent["sq"].wait_send()
    got("rs", "kv")
    for half in range(2):
        @pl.loop(0, toks // RT)
        def _(i):
            at_rows = pl.ds(pl.multiple_of(i * RT, RT), RT)
            scale = inv[half, at_rows, :]
            total = jnp.sum(rs[half, at_rows, :] + rs_in[1 - half, at_rows, :], axis=1, keepdims=True)
            sq[half, at_rows, :] = (jnp.broadcast_to(total, (RT, lanes)) * scale / features) * scale * scale
            if half == 0:
                whole = kvp[0, at_rows, :] + kvx[at_rows, :]
                cots[0, at_rows, :] = (whole * wide(scale, cols)).astype(bf16)

    store_kv = pltpu.make_async_copy(cots.at[0], kv_out, local_sem.at[2 * blocks + 2])
    store_kv.start()

    back_loop(0, 2)
    reduce_b_opposite()
    reduce_a(0)
    back_loop(2, 5)
    got("ra_r1", "ra_l1")
    add_rows(RA, far, 0, (ra_x, (0,)), (ra_x, (1,)))
    send("za", u.at[far, a_rows], za_out, partner)
    reduce_b_side()
    back_loop(5, 8)
    got("rz3")
    add_rows(RB, own, RA, (rb_z, (3,)))

    store_own = load(u.at[own], own_out, 2 * blocks + 3)
    store_kv.wait()
    got("rb_r", "rb_l", "ra_r0", "ra_l0", "za")
    for name, copy in sent.items():
        if name != "sq":
            copy.wait_send()

    @pl.loop(0, blocks)
    def _(k):
        ig_store(k).wait()
        ig_send(k).wait()

    store_drift.wait()
    store_own.wait()


def layer(tokens, weight, gain, cotangent, outer, inner, order):
    toks, features = tokens.shape
    rows, cols = weight.shape
    blocks = features // rows // 2
    RA, RB, HA, HB = split_rows(rows)
    lanes = min(LANES, rows)
    any_space = pl.BlockSpec(memory_space=pl.ANY)
    vector = pltpu.VMEM((2, toks, lanes), f32)
    return pl.pallas_call(
        functools.partial(layer_kernel, features),
        out_shape=(
            jax.ShapeDtypeStruct((toks, cols), bf16),
            jax.ShapeDtypeStruct((toks, features), bf16),
            jax.ShapeDtypeStruct((rows, cols), bf16),
            jax.ShapeDtypeStruct((2, RA, cols), bf16),
            jax.ShapeDtypeStruct((RA, cols), bf16),
            jax.ShapeDtypeStruct((2, RB, cols), bf16),
            jax.ShapeDtypeStruct(inner.shape, f32),
        ),
        in_specs=[pl.BlockSpec(memory_space=pltpu.SMEM), pl.BlockSpec(memory_space=pltpu.VMEM)]
        + [any_space] * 5,
        out_specs=(any_space,) * 7,
        scratch_shapes=[
            pltpu.VMEM((2, blocks, toks, rows), bf16),
            pltpu.VMEM((blocks, rows, cols), bf16),
            pltpu.VMEM((blocks, rows, cols), bf16),
            pltpu.VMEM((2, toks, cols), bf16),
            pltpu.VMEM((2, toks, cols), bf16),
            pltpu.VMEM((2, toks, cols), f32),
            pltpu.VMEM((toks, cols), f32),
            vector, vector, vector, vector, vector,
            pltpu.VMEM((2, 2, max(HA, RA - HA), cols), bf16),
            pltpu.VMEM((4, RB, cols), bf16),
            pltpu.VMEM((2, max(HB, RB - HB), cols), bf16),
            pltpu.VMEM((2, RA, cols), bf16),
            pltpu.VMEM(outer.shape, f32),
            pltpu.VMEM(inner.shape, f32),
            pltpu.VMEM(inner.shape, bf16),
            pltpu.VMEM(inner.shape, bf16),
            pltpu.VMEM(inner.shape, f32),
            pltpu.VMEM((2, inner.shape[0] // 4, inner.shape[1]), f32),
            pltpu.SemaphoreType.DMA((72,)),
            pltpu.SemaphoreType.DMA((72,)),
            pltpu.SemaphoreType.DMA((32,)),
        ],
        compiler_params=pltpu.CompilerParams(
            collective_id=0, has_side_effects=True, vmem_limit_bytes=60 * 1024 * 1024
        ),
        cost_estimate=pl.CostEstimate(
            flops=6 * toks * features * cols, bytes_accessed=400 * 1024 * 1024, transcendentals=0
        ),
        name="layer",
    )(order, gain, tokens, weight, cotangent, outer, inner)


PIECES = 8


def finish_kernel(
    replicas, order, gain, ig_in, kv_in, own_in, xa_in, za_in, xb_in, drift_in, w_in, outer_in, moment_in,
    kv_out, ig_out, wg_out, gg_out, outer_out, moment_out,
    ig, kv, own, xa, za, xb, u, w, column, partial, share, drift, outer, moment, sem,
):
    rows, cols = u.shape
    lanes = min(LANES, rows)
    started = []

    def copy(src, dst):
        move = pltpu.make_async_copy(src, dst, sem.at[len(started)])
        move.start()
        started.append(move)
        return move

    terms = [copy(own_in, own), copy(w_in, w), copy(xa_in, xa), copy(za_in, za), copy(xb_in, xb)]
    get_drift, get_outer, get_moment = copy(drift_in, drift), copy(outer_in, outer), copy(moment_in, moment)
    step = ig_in.shape[0] // PIECES
    pieces = [pl.ds(i * step, step) for i in range(PIECES)]
    gets = [copy(kv_in, kv)] + [copy(ig_in.at[p], ig.at[p]) for p in pieces]
    puts = [(kv, kv_out)] + [(ig.at[p], ig_out.at[p]) for p in pieces]
    moves = []

    def pass_on(count):
        for _ in range(count):
            gets.pop(0).wait()
            moves.append(copy(*puts.pop(0)))

    column[...] = jnp.broadcast_to(gain[...].astype(f32), (lanes, rows)).T
    for term in terms:
        term.wait()
    RT = 32
    first = za.shape[0]

    def last_sum(lo, count, *others):
        @pl.loop(0, count // RT)
        def _(i):
            at_rows = pl.ds(pl.multiple_of(lo + i * RT, RT), RT)
            there = pl.ds(pl.multiple_of(i * RT, RT), RT)
            whole = own[at_rows, :].astype(f32)
            for ref, index in others:
                whole = whole + ref[(*index, there, slice(None))].astype(f32)
            product = whole * w[at_rows, :].astype(f32)
            total = product[:, :lanes]
            for j in range(1, cols // lanes):
                total = total + product[:, j * lanes : (j + 1) * lanes]
            partial[at_rows, :] = total
            u[at_rows, :] = whole * jnp.concatenate([column[at_rows, :]] * (cols // lanes), axis=1)

    last_sum(0, first, (xa, (0,)), (xa, (1,)), (za, ()))
    last_sum(first, rows - first, (xb, (0,)), (xb, (1,)))
    moves.append(copy(u, wg_out))
    pass_on(3)
    share[...] = jnp.sum(partial[...].T, axis=0, keepdims=True)
    moves.append(copy(share, gg_out))
    pass_on(2)
    get_drift.wait()
    get_outer.wait()
    get_moment.wait()
    now = order[0]
    averaged = drift[...] / replicas
    fresh = outer_beta * moment[now] + averaged
    moment[now] = fresh
    outer[now] = outer[now] - outer_rate * (averaged + outer_beta * fresh)
    moves.append(copy(moment, moment_out))
    moves.append(copy(outer, outer_out))
    pass_on(len(gets))
    for move in moves:
        move.wait()


def finish(replicas, order, ig, kv, terms, drift, weight, gain, outer, moment):
    rows, cols = weight.shape
    lanes = min(LANES, rows)
    any_space = pl.BlockSpec(memory_space=pl.ANY)
    return pl.pallas_call(
        functools.partial(finish_kernel, replicas),
        out_shape=(
            jax.ShapeDtypeStruct(kv.shape, bf16),
            jax.ShapeDtypeStruct(ig.shape, bf16),
            jax.ShapeDtypeStruct((rows, cols), f32),
            jax.ShapeDtypeStruct(gain.shape, f32),
            jax.ShapeDtypeStruct(outer.shape, f32),
            jax.ShapeDtypeStruct(moment.shape, f32),
        ),
        in_specs=[pl.BlockSpec(memory_space=pltpu.SMEM), pl.BlockSpec(memory_space=pltpu.VMEM)]
        + [any_space] * 10,
        out_specs=(any_space,) * 6,
        scratch_shapes=[
            pltpu.VMEM(ig.shape, bf16),
            pltpu.VMEM(kv.shape, bf16),
            *(pltpu.VMEM(term.shape, bf16) for term in terms),
            pltpu.VMEM((rows, cols), f32),
            pltpu.VMEM((rows, cols), bf16),
            pltpu.VMEM((rows, lanes), f32),
            pltpu.VMEM((rows, lanes), f32),
            pltpu.VMEM(gain.shape, f32),
            pltpu.VMEM(drift.shape, f32),
            pltpu.VMEM(outer.shape, f32),
            pltpu.VMEM(moment.shape, f32),
            pltpu.SemaphoreType.DMA((32,)),
        ],
        compiler_params=pltpu.CompilerParams(vmem_limit_bytes=60 * 1024 * 1024),
        name="finish",
    )(order, gain, ig, kv, *terms, drift, weight, outer, moment)


def on_device(
    tokens, kv_weight, norm_gain, cotangent, global_params, momentum, local_params, fragment_order
):
    weight = kv_weight[0]
    kv, ig, *terms, drift = layer(
        tokens, weight, norm_gain, cotangent, global_params, local_params[0], fragment_order
    )
    keys_values, input_grad, weight_grad, gain_grad, new_params, new_momentum = finish(
        lax.axis_size("replica"), fragment_order, ig, kv, terms, drift, weight, norm_gain, global_params, momentum
    )
    return (keys_values, input_grad, weight_grad[None], gain_grad, new_params, new_momentum)


def solution(mesh):
    return jax.shard_map(
        on_device,
        mesh=mesh,
        in_specs=(
            P(("replica", "fsdp"), None),
            P("replica", "fsdp", None),
            P("replica", "fsdp"),
            P(("replica", "fsdp"), None),
            P(None, "fsdp", None),
            P(None, "fsdp", None),
            P("replica", "fsdp", None),
            P(),
        ),
        out_specs=(
            P(("replica", "fsdp"), None),
            P(("replica", "fsdp"), None),
            P("replica", "fsdp", None),
            P("replica", "fsdp"),
            P(None, "fsdp", None),
            P(None, "fsdp", None),
        ),
        check_vma=False,
    )
```

```python
import functools

import jax
import jax.numpy as jnp
from jax import lax
from jax.experimental import pallas as pl
from jax.experimental.pallas import tpu as pltpu
from jax.sharding import PartitionSpec as P

epsilon = 1e-05
outer_beta = 0.9
outer_rate = 0.7
f32 = jnp.float32
bf16 = jnp.bfloat16
MESH = pl.DeviceIdType.MESH
LANES = 128


def split_rows(rows):
    first = max(32, rows * 9 // 16 // 32 * 32)
    return first, rows - first, first // 2, (rows - first) // 2


def layer_kernel(
    features, order, gain, tok_hbm, w_hbm, cot_hbm, outer_hbm, inner_hbm,
    kv_out, ig_out, own_out, xa_out, za_out, xb_out, drift_out,
    tok, w, u, cot, cots, kvp, kvx, sq, sq_in, inv, rs, rs_in,
    ra_opp, rb_z, rb_opp, ra_x,
    outer, inner, drift, drift_in, drifts, drifts_in, send_sem, recv_sem, local_sem,
):
    rows, cols = w_hbm.shape
    toks = tok_hbm.shape[0]
    RA, RB, HA, HB = split_rows(rows)
    r = lax.axis_index("replica")
    me = lax.axis_index("fsdp")
    zh = lax.div(me, 8)
    x = lax.rem(lax.div(me, 2), 4)
    c = lax.rem(me, 2)

    def at(plane, col, core):
        return (r, plane * 8 + col * 2 + core)

    right = at(zh, lax.rem(x + 1, 4), c)
    left = at(zh, lax.rem(x + 3, 4), c)
    partner = at(1 - zh, x, c)
    sibling = at(zh, x, 1 - c)
    z_lo, y = lax.div(r, 4), lax.rem(r, 4)
    peers = (
        ((1 - z_lo) * 4 + y, me),
        (z_lo * 4 + y + 1 - 2 * lax.rem(y, 2), me),
        (z_lo * 4 + 3 - y, me),
    )

    def slot(plane, dx):
        return (zh if plane == 0 else 1 - zh) * 4 + lax.rem(x + dx + 4, 4)

    blocks = features // rows // 2

    def columns(k, core):
        return pl.ds(pl.multiple_of((2 * k + core) * rows, rows), rows)

    barrier = pltpu.get_barrier_semaphore()
    around = (right, left, partner, sibling, *peers)
    for other in around:
        pl.semaphore_signal(barrier, inc=1, device_id=other, device_id_type=MESH)
    early = 2 * blocks + 5

    def load(src, dst, i):
        copy = pltpu.make_async_copy(src, dst, local_sem.at[i])
        copy.start()
        return copy

    load_w = load(w_hbm, cots.at[0], early)
    loads = [load(tok_hbm.at[:, columns(k, c)], tok.at[0, k], k) for k in range(blocks)]
    load_cot = load(cot_hbm, cot.at[0], blocks)
    load_outer = load(outer_hbm, outer, early + 2)
    load_inner = load(inner_hbm, inner, early + 3)
    pl.semaphore_wait(barrier, len(around))

    sent = {}

    def send(name, src, dst, to):
        i = len(sent)
        copy = pltpu.make_async_remote_copy(
            src_ref=src, dst_ref=dst, send_sem=send_sem.at[i], recv_sem=recv_sem.at[i],
            device_id=to, device_id_type=MESH,
        )
        copy.start()
        sent[name] = copy

    def got(*names):
        for name in names:
            sent[name].wait_recv()

    a_rows, b_rows = pl.ds(0, RA), pl.ds(RA, RB)
    a_first, a_last = pl.ds(0, HA), pl.ds(HA, RA - HA)
    b_first, b_last = pl.ds(RA, HB), pl.ds(RA + HB, RB - HB)

    own = slot(0, 0)
    lanes = min(LANES, rows)
    AT = 16

    def wide(column, width):
        return jnp.concatenate([column] * (width // lanes), axis=1) if width > lanes else column[:, :width]

    def gained(lo, count):
        @pl.loop(0, count // AT)
        def _(i):
            to = pl.ds(pl.multiple_of(lo + i * AT, AT), AT)
            w[own, to, :] = (cots[0, to, :].astype(f32) * wide(rs[0, to, :], cols)).astype(bf16)

    rs[0, pl.ds(0, rows), :] = jnp.broadcast_to(gain[...].astype(f32), (lanes, rows)).T
    load_w.wait()
    gained(RA, RB)
    send("g_right_b", w.at[own, b_rows], w.at[own, b_rows], right)
    send("g_left_b", w.at[own, b_rows], w.at[own, b_rows], left)
    gained(0, RA)
    send("g_z_a", w.at[own, a_rows], w.at[own, a_rows], partner)
    send("g_right_a", w.at[own, a_rows], w.at[own, a_rows], right)
    send("g_left_a", w.at[own, a_rows], w.at[own, a_rows], left)
    send("g_z_b", w.at[own, b_rows], w.at[own, b_rows], partner)
    for k in range(blocks):
        send(f"t{k}", tok_hbm.at[:, columns(k, 1 - c)], tok.at[1, k], sibling)
    send("cot", cot_hbm, cot.at[1], sibling)

    load_outer.wait()
    load_inner.wait()
    drift[...] = (outer[order[0]] - inner[...]).astype(bf16)
    n_half, n_quarter = drift.shape[0] // 2, drift.shape[0] // 4
    keep = lax.rem(y + lax.div(y, 2), 2)
    upper = lax.div(y, 2)
    half_at = pl.multiple_of(keep * n_half, n_half)
    quarter_at = pl.multiple_of(half_at + upper * n_quarter, n_quarter)
    my_half, my_quarter = pl.ds(half_at, n_half), pl.ds(quarter_at, n_quarter)
    other_half = pl.ds(pl.multiple_of((1 - keep) * n_half, n_half), n_half)
    other_quarter = pl.ds(pl.multiple_of(half_at + (1 - upper) * n_quarter, n_quarter), n_quarter)
    send("d0", drift.at[other_half], drift_in.at[pl.ds(0, n_half)], peers[1])

    def drift_step(step):
        got(f"d{step}")
        if step == 0:
            mine_in = pl.ds(pl.multiple_of(upper * n_quarter, n_quarter), n_quarter)
            other_in = pl.ds(pl.multiple_of((1 - upper) * n_quarter, n_quarter), n_quarter)
            drifts[my_quarter, :] = drift[my_quarter, :].astype(f32) + drift_in[mine_in, :].astype(f32)
            drifts_in[0] = drift[other_quarter, :].astype(f32) + drift_in[other_in, :].astype(f32)
            send("d1", drifts_in.at[0], drifts_in.at[1], peers[2])
        elif step == 1:
            total = (drifts[my_quarter, :] + drifts_in[1]).astype(bf16)
            drift_in[pl.ds(n_half, n_quarter), :] = total
            send("d2", drift_in.at[pl.ds(n_half, n_quarter)], drift_in.at[pl.ds(n_half + n_quarter, n_quarter)], peers[0])
        elif step == 2:
            drifts[my_quarter, :] = (
                drift_in[pl.ds(n_half, n_quarter), :].astype(f32)
                + drift_in[pl.ds(n_half + n_quarter, n_quarter), :].astype(f32)
            )
            send("d3", drifts.at[my_quarter], drifts.at[my_quarter], peers[2])
        elif step == 3:
            send("d4", drifts.at[my_half], drifts.at[my_half], peers[1])

    RT = min(64, toks)

    def square_block(half, k, fresh):
        @pl.loop(0, toks // RT)
        def _(i):
            at_rows = pl.ds(pl.multiple_of(i * RT, RT), RT)
            piece = tok[half, k, at_rows, :].astype(f32)
            piece = piece * piece
            total = piece[:, :lanes]
            for j in range(1, rows // lanes):
                total = total + piece[:, j * lanes : (j + 1) * lanes]
            if fresh:
                sq[half, at_rows, :] = total
            else:
                sq[half, at_rows, :] += total

    for half in range(2):
        for k in range(blocks):
            if half == 0:
                loads[k].wait()
            else:
                got(f"t{k}")
            square_block(half, k, k == 0)
    send("sq", sq, sq_in, sibling)
    load_cot.wait()
    got("cot", "sq")

    for half in range(2):
        @pl.loop(0, toks // RT)
        def _(i):
            at_rows = pl.ds(pl.multiple_of(i * RT, RT), RT)
            total = sq[half, at_rows, :] + sq_in[1 - half, at_rows, :]
            mean = jnp.sum(total, axis=1, keepdims=True) / features
            root = jnp.broadcast_to(lax.rsqrt(mean + epsilon), (RT, lanes))
            inv[half, at_rows, :] = root
            cots[half, at_rows, :] = (cot[half, at_rows, :].astype(f32) * wide(root, cols)).astype(bf16)

    FT = min(256, rows)
    TT = min(256, toks)

    def u_block(k):
        @pl.loop(0, rows // FT)
        def _(j):
            at_rows = pl.ds(pl.multiple_of(j * FT, FT), FT)
            total = None
            for half in range(2):
                term = lax.dot_general(
                    tok[half, k, :, at_rows], cots[half], (((0,), (0,)), ((), ())),
                    preferred_element_type=f32,
                )
                total = term if total is None else total + term
            u[k, at_rows, :] = total.astype(bf16)

    def kv_block(k, fresh=False):
        for half in range(2):
            @pl.loop(0, toks // TT)
            def _(j):
                at_rows = pl.ds(pl.multiple_of(j * TT, TT), TT)
                term = jnp.dot(tok[half, k, at_rows, :], w[k], preferred_element_type=f32)
                if fresh:
                    kvp[half, at_rows, :] = term
                else:
                    kvp[half, at_rows, :] += term

    def back_block(k):
        for half in range(2):
            @pl.loop(0, toks // TT)
            def _(j):
                at_rows = pl.ds(pl.multiple_of(j * TT, TT), TT)
                weighted = lax.dot_general(
                    cot[half, at_rows, :], w[k], (((1,), (1,)), ((), ())),
                    preferred_element_type=f32,
                )
                grad = weighted * wide(inv[half, at_rows, :], rows) - tok[
                    half, k, at_rows, :
                ].astype(f32) * wide(sq[half, at_rows, :], rows)
                tok[half, k, at_rows, :] = grad.astype(bf16)

    ig_base = 64

    def ig_store(k):
        return pltpu.make_async_copy(
            tok.at[0, k], ig_out.at[:, columns(k, c)], local_sem.at[blocks + 2 + k]
        )

    def ig_send(k):
        return pltpu.make_async_remote_copy(
            src_ref=tok.at[1, k], dst_ref=ig_out.at[:, columns(k, c)],
            send_sem=send_sem.at[ig_base + k], recv_sem=recv_sem.at[ig_base + k],
            device_id=sibling, device_id_type=MESH,
        )

    def back_loop(lo, hi):
        @pl.loop(lo, hi)
        def _(k):
            back_block(k)
            ig_store(k).start()
            ig_send(k).start()

    def add_rows(count, dst, dst_at, *srcs):
        @pl.loop(0, count // AT)
        def _(i):
            to = pl.ds(pl.multiple_of(dst_at + i * AT, AT), AT)
            total = u[dst, to, :].astype(f32)
            for ref, index in srcs:
                total = total + ref[(*index, pl.ds(pl.multiple_of(i * AT, AT), AT), slice(None))].astype(f32)
            u[dst, to, :] = total.astype(bf16)

    def reduce_a(plane):
        got(f"ro_r{plane}", f"ro_l{plane}")
        to_right, to_left = slot(plane, 1), slot(plane, -1)
        add_rows(HA, to_right, 0, (ra_opp, (0, plane)))
        land = xa_out if plane == 0 else ra_x
        send(f"ra_r{plane}", u.at[to_right, a_rows], land.at[0], right)
        add_rows(RA - HA, to_left, HA, (ra_opp, (1, plane)))
        send(f"ra_l{plane}", u.at[to_left, a_rows], land.at[1], left)

    def reduce_b_opposite():
        got("rz0")
        add_rows(RB, mine_o, RA, (rb_z, (0,)))
        send("rbo_r", u.at[mine_o, b_first], rb_opp.at[0, pl.ds(0, HB)], right)
        send("rbo_l", u.at[mine_o, b_last], rb_opp.at[1, pl.ds(0, RB - HB)], left)
        got("rz1")
        add_rows(RB, mine_r, RA, (rb_z, (1,)))
        got("rz2")
        add_rows(RB, mine_l, RA, (rb_z, (2,)))

    def reduce_b_side():
        got("rbo_r", "rbo_l")
        add_rows(HB, mine_r, RA, (rb_opp, (0,)))
        send("rb_r", u.at[mine_r, b_rows], xb_out.at[0], right)
        add_rows(RB - HB, mine_l, RA + HB, (rb_opp, (1,)))
        send("rb_l", u.at[mine_l, b_rows], xb_out.at[1], left)

    def u_loop(lo, hi):
        @pl.loop(lo, hi)
        def _(k):
            u_block(k)

    mine_r, mine_l, mine_o = slot(0, 1), slot(0, -1), slot(0, 2)
    far, far_r, far_l, far_o = slot(1, 0), slot(1, 1), slot(1, -1), slot(1, 2)
    got("g_right_b", "g_left_b", "g_z_a")
    send("g2_right_b", w.at[mine_l, b_first], w.at[mine_l, b_first], right)
    send("g2_left_b", w.at[mine_r, b_last], w.at[mine_r, b_last], left)
    send("gz_l", w.at[mine_l, b_rows], w.at[mine_l, b_rows], partner)
    send("gz_r", w.at[mine_r, b_rows], w.at[mine_r, b_rows], partner)
    send("h_right_a", w.at[far, a_rows], w.at[far, a_rows], right)
    send("h_left_a", w.at[far, a_rows], w.at[far, a_rows], left)
    u_loop(0, 3)
    drift_step(0)
    got("g_right_a", "g_left_a")
    send("g2_right_a", w.at[mine_l, a_first], w.at[mine_l, a_first], right)
    send("g2_left_a", w.at[mine_r, a_last], w.at[mine_r, a_last], left)
    u_loop(3, 6)
    drift_step(1)
    got("g2_right_b", "g2_left_b")
    send("gz_o", w.at[mine_o, b_rows], w.at[mine_o, b_rows], partner)
    u_loop(6, 8)
    for j, dx in enumerate((2, 1, -1, 0)):
        send(f"rz{j}", u.at[slot(1, dx), b_rows], rb_z.at[j], partner)
    kv_block(own, True)
    drift_step(2)

    @pl.loop(0, 2)
    def _(i):
        kv_block(zh * 4 + lax.rem(x + 1 + 2 * i, 4))

    got("h_right_a", "h_left_a")
    send("h2_right_a", w.at[far_l, a_first], w.at[far_l, a_first], right)
    send("h2_left_a", w.at[far_r, a_last], w.at[far_r, a_last], left)
    for plane in (1, 0):
        opp = slot(plane, 2)
        send(f"ro_r{plane}", u.at[opp, a_first], ra_opp.at[0, plane, pl.ds(0, HA)], right)
        send(f"ro_l{plane}", u.at[opp, a_last], ra_opp.at[1, plane, pl.ds(0, RA - HA)], left)
    drift_step(3)
    got("g2_right_a", "g2_left_a", "g_z_b")
    kv_block(mine_o)
    kv_block(far)
    got("gz_l", "gz_r", "h2_right_a", "h2_left_a", "gz_o")

    @pl.loop(1, 4)
    def _(i):
        kv_block((1 - zh) * 4 + lax.rem(x + i, 4))

    send("kv", kvp.at[1], kvx, sibling)
    for half in range(2):
        @pl.loop(0, toks // RT)
        def _(i):
            at_rows = pl.ds(pl.multiple_of(i * RT, RT), RT)
            piece = kvp[half, at_rows, :] * cot[half, at_rows, :].astype(f32)
            total = piece[:, :lanes]
            for j in range(1, cols // lanes):
                total = total + piece[:, j * lanes : (j + 1) * lanes]
            rs[half, at_rows, :] = total

    send("rs", rs, rs_in, sibling)
    got("d4")
    store_drift = load(drifts, drift_out, early)
    reduce_a(1)
    sent["sq"].wait_send()
    got("rs", "kv")
    for half in range(2):
        @pl.loop(0, toks // RT)
        def _(i):
            at_rows = pl.ds(pl.multiple_of(i * RT, RT), RT)
            scale = inv[half, at_rows, :]
            total = jnp.sum(rs[half, at_rows, :] + rs_in[1 - half, at_rows, :], axis=1, keepdims=True)
            sq[half, at_rows, :] = (jnp.broadcast_to(total, (RT, lanes)) * scale / features) * scale * scale
            if half == 0:
                whole = kvp[0, at_rows, :] + kvx[at_rows, :]
                cots[0, at_rows, :] = (whole * wide(scale, cols)).astype(bf16)

    store_kv = pltpu.make_async_copy(cots.at[0], kv_out, local_sem.at[2 * blocks + 2])
    store_kv.start()

    back_loop(0, 2)
    reduce_b_opposite()
    reduce_a(0)
    back_loop(2, 5)
    got("ra_r1", "ra_l1")
    add_rows(RA, far, 0, (ra_x, (0,)), (ra_x, (1,)))
    send("za", u.at[far, a_rows], za_out, partner)
    reduce_b_side()
    back_loop(5, 8)
    got("rz3")
    add_rows(RB, own, RA, (rb_z, (3,)))

    store_own = load(u.at[own], own_out, 2 * blocks + 3)
    store_kv.wait()
    got("rb_r", "rb_l", "ra_r0", "ra_l0", "za")
    for name, copy in sent.items():
        if name != "sq":
            copy.wait_send()

    @pl.loop(0, blocks)
    def _(k):
        ig_store(k).wait()
        ig_send(k).wait()

    store_drift.wait()
    store_own.wait()


def layer(tokens, weight, gain, cotangent, outer, inner, order):
    toks, features = tokens.shape
    rows, cols = weight.shape
    blocks = features // rows // 2
    RA, RB, HA, HB = split_rows(rows)
    lanes = min(LANES, rows)
    any_space = pl.BlockSpec(memory_space=pl.ANY)
    vector = pltpu.VMEM((2, toks, lanes), f32)
    return pl.pallas_call(
        functools.partial(layer_kernel, features),
        out_shape=(
            jax.ShapeDtypeStruct((toks, cols), bf16),
            jax.ShapeDtypeStruct((toks, features), bf16),
            jax.ShapeDtypeStruct((rows, cols), bf16),
            jax.ShapeDtypeStruct((2, RA, cols), bf16),
            jax.ShapeDtypeStruct((RA, cols), bf16),
            jax.ShapeDtypeStruct((2, RB, cols), bf16),
            jax.ShapeDtypeStruct(inner.shape, f32),
        ),
        in_specs=[pl.BlockSpec(memory_space=pltpu.SMEM), pl.BlockSpec(memory_space=pltpu.VMEM)]
        + [any_space] * 5,
        out_specs=(any_space,) * 7,
        scratch_shapes=[
            pltpu.VMEM((2, blocks, toks, rows), bf16),
            pltpu.VMEM((blocks, rows, cols), bf16),
            pltpu.VMEM((blocks, rows, cols), bf16),
            pltpu.VMEM((2, toks, cols), bf16),
            pltpu.VMEM((2, toks, cols), bf16),
            pltpu.VMEM((2, toks, cols), f32),
            pltpu.VMEM((toks, cols), f32),
            vector, vector, vector, vector, vector,
            pltpu.VMEM((2, 2, max(HA, RA - HA), cols), bf16),
            pltpu.VMEM((4, RB, cols), bf16),
            pltpu.VMEM((2, max(HB, RB - HB), cols), bf16),
            pltpu.VMEM((2, RA, cols), bf16),
            pltpu.VMEM(outer.shape, f32),
            pltpu.VMEM(inner.shape, f32),
            pltpu.VMEM(inner.shape, bf16),
            pltpu.VMEM(inner.shape, bf16),
            pltpu.VMEM(inner.shape, f32),
            pltpu.VMEM((2, inner.shape[0] // 4, inner.shape[1]), f32),
            pltpu.SemaphoreType.DMA((72,)),
            pltpu.SemaphoreType.DMA((72,)),
            pltpu.SemaphoreType.DMA((32,)),
        ],
        compiler_params=pltpu.CompilerParams(
            collective_id=0, has_side_effects=True, vmem_limit_bytes=47 * 1024 * 1024
        ),
        cost_estimate=pl.CostEstimate(
            flops=6 * toks * features * cols, bytes_accessed=400 * 1024 * 1024, transcendentals=0
        ),
        name="layer",
    )(order, gain, tokens, weight, cotangent, outer, inner)


PIECES = 8


def finish_kernel(
    replicas, order, gain, ig_in, kv_in, own_in, xa_in, za_in, xb_in, drift_in, w_in, outer_in, moment_in,
    kv_out, ig_out, wg_out, gg_out, outer_out, moment_out,
    ig, kv, own, xa, za, xb, u, w, column, partial, share, drift, outer, moment, sem,
):
    rows, cols = u.shape
    lanes = min(LANES, rows)
    started = []

    def copy(src, dst):
        move = pltpu.make_async_copy(src, dst, sem.at[len(started)])
        move.start()
        started.append(move)
        return move

    terms = [copy(own_in, own), copy(w_in, w), copy(xa_in, xa), copy(za_in, za), copy(xb_in, xb)]
    get_drift, get_outer, get_moment = copy(drift_in, drift), copy(outer_in, outer), copy(moment_in, moment)
    step = ig_in.shape[0] // PIECES
    pieces = [pl.ds(i * step, step) for i in range(PIECES)]
    gets = [copy(kv_in, kv)] + [copy(ig_in.at[p], ig.at[p]) for p in pieces]
    puts = [(kv, kv_out)] + [(ig.at[p], ig_out.at[p]) for p in pieces]
    moves = []

    def pass_on(count):
        for _ in range(count):
            gets.pop(0).wait()
            moves.append(copy(*puts.pop(0)))

    column[...] = jnp.broadcast_to(gain[...].astype(f32), (lanes, rows)).T
    for term in terms:
        term.wait()
    RT = 32
    first = za.shape[0]

    def last_sum(lo, count, *others):
        @pl.loop(0, count // RT)
        def _(i):
            at_rows = pl.ds(pl.multiple_of(lo + i * RT, RT), RT)
            there = pl.ds(pl.multiple_of(i * RT, RT), RT)
            whole = own[at_rows, :].astype(f32)
            for ref, index in others:
                whole = whole + ref[(*index, there, slice(None))].astype(f32)
            product = whole * w[at_rows, :].astype(f32)
            total = product[:, :lanes]
            for j in range(1, cols // lanes):
                total = total + product[:, j * lanes : (j + 1) * lanes]
            partial[at_rows, :] = total
            u[at_rows, :] = whole * jnp.concatenate([column[at_rows, :]] * (cols // lanes), axis=1)

    last_sum(0, first, (xa, (0,)), (xa, (1,)), (za, ()))
    last_sum(first, rows - first, (xb, (0,)), (xb, (1,)))
    moves.append(copy(u, wg_out))
    pass_on(3)
    share[...] = jnp.sum(partial[...].T, axis=0, keepdims=True)
    moves.append(copy(share, gg_out))
    pass_on(2)
    get_drift.wait()
    get_outer.wait()
    get_moment.wait()
    now = order[0]
    averaged = drift[...] / replicas
    fresh = outer_beta * moment[now] + averaged
    moment[now] = fresh
    outer[now] = outer[now] - outer_rate * (averaged + outer_beta * fresh)
    moves.append(copy(moment, moment_out))
    moves.append(copy(outer, outer_out))
    pass_on(len(gets))
    for move in moves:
        move.wait()


def finish(replicas, order, ig, kv, terms, drift, weight, gain, outer, moment):
    rows, cols = weight.shape
    lanes = min(LANES, rows)
    any_space = pl.BlockSpec(memory_space=pl.ANY)
    return pl.pallas_call(
        functools.partial(finish_kernel, replicas),
        out_shape=(
            jax.ShapeDtypeStruct(kv.shape, bf16),
            jax.ShapeDtypeStruct(ig.shape, bf16),
            jax.ShapeDtypeStruct((rows, cols), f32),
            jax.ShapeDtypeStruct(gain.shape, f32),
            jax.ShapeDtypeStruct(outer.shape, f32),
            jax.ShapeDtypeStruct(moment.shape, f32),
        ),
        in_specs=[pl.BlockSpec(memory_space=pltpu.SMEM), pl.BlockSpec(memory_space=pltpu.VMEM)]
        + [any_space] * 10,
        out_specs=(any_space,) * 6,
        scratch_shapes=[
            pltpu.VMEM(ig.shape, bf16),
            pltpu.VMEM(kv.shape, bf16),
            *(pltpu.VMEM(term.shape, bf16) for term in terms),
            pltpu.VMEM((rows, cols), f32),
            pltpu.VMEM((rows, cols), bf16),
            pltpu.VMEM((rows, lanes), f32),
            pltpu.VMEM((rows, lanes), f32),
            pltpu.VMEM(gain.shape, f32),
            pltpu.VMEM(drift.shape, f32),
            pltpu.VMEM(outer.shape, f32),
            pltpu.VMEM(moment.shape, f32),
            pltpu.SemaphoreType.DMA((32,)),
        ],
        compiler_params=pltpu.CompilerParams(vmem_limit_bytes=50 * 1024 * 1024),
        name="finish",
    )(order, gain, ig, kv, *terms, drift, weight, outer, moment)


def on_device(
    tokens, kv_weight, norm_gain, cotangent, global_params, momentum, local_params, fragment_order
):
    weight = kv_weight[0]
    kv, ig, *terms, drift = layer(
        tokens, weight, norm_gain, cotangent, global_params, local_params[0], fragment_order
    )
    keys_values, input_grad, weight_grad, gain_grad, new_params, new_momentum = finish(
        lax.axis_size("replica"), fragment_order, ig, kv, terms, drift, weight, norm_gain, global_params, momentum
    )
    return (keys_values, input_grad, weight_grad[None], gain_grad, new_params, new_momentum)


def solution(mesh):
    return jax.shard_map(
        on_device,
        mesh=mesh,
        in_specs=(
            P(("replica", "fsdp"), None),
            P("replica", "fsdp", None),
            P("replica", "fsdp"),
            P(("replica", "fsdp"), None),
            P(None, "fsdp", None),
            P(None, "fsdp", None),
            P("replica", "fsdp", None),
            P(),
        ),
        out_specs=(
            P(("replica", "fsdp"), None),
            P(("replica", "fsdp"), None),
            P("replica", "fsdp", None),
            P("replica", "fsdp"),
            P(None, "fsdp", None),
            P(None, "fsdp", None),
        ),
        check_vma=False,
    )
```
